128 devices in a mesh: grp: 8 (over x, core), tp: 16 (over y, z).
Axes of the slice: x: 4, y: 4, z: 4, core: 2. Of those that a mesh axis runs over, the one named last changes fastest.
Arguments:
- tokens: bfloat16 [12288, 8192], P(('grp', 'tp')), may hold values from -6 to 6
- holder: int32 [12288, 1], P(('grp', 'tp')), may hold values from 0 to 127; in each aligned block of 96 rows (0 to 95, 96 to 191, ...) at most 2 rows name the same one
- adapter_choice_index: int32 [12288, 1], P(('grp', 'tp')), may hold values from 0 to 1
- query_base_output: bfloat16 [8192, 8192], P(None, 'tp'), may hold values from -0.0625 to 0.0625
- value_base_output: bfloat16 [8192, 1024], P(None, 'tp'), may hold values from -0.0625 to 0.0625
- adapter_down_weight: bfloat16 [256, 8192, 128], P(('grp', 'tp')), may hold values from -0.0625 to 0.0625
- adapter_query_up: bfloat16 [256, 64, 8192], P(('grp', 'tp')), may hold values from -0.75 to 0.75
- adapter_value_up: bfloat16 [256, 64, 1024], P(('grp', 'tp')), may hold values from -0.75 to 0.75
Outputs:
- queries: bfloat16 [12288, 8192], P(('grp', 'tp'))
- values: bfloat16 [12288, 1024], P(('grp', 'tp'))
The draws below stay inside these ranges and needn't reach their ends.
Inputs may be any that keep to these rules, and one draw needn't show every extreme that they name: Among the 96 requests of one device no holder appears more than 2 times, and some holder appears exactly 2 times.
All inputs are finite; a program needn't handle non-finite values.
Results may differ from the reference program's by a relative error of at most 0.0057.
Values may be sent and summed in bfloat16 or wider, within the bound.
No kernel may reach another device: no remote copies, remote signals or barrier semaphores. Data moves between devices by JAX's collectives and lax.ppermute only.
A program may use at most 128 MiB of HBM per device.

```python
import math
import jax
import jax.numpy as jnp
import numpy as np
from jax import lax

MODEL_WIDTH = 8192
DQ = 8192
DV = 1024
ADAPTER_RANK = 64
TEN_DEV = 2
TOK_DEV = 96
CAP = 2
ROWS = 12288
ADAPTER_TOTAL = 256
N_GRP = 8
N_TP = 16


def set_ends(result, own_key, least, high):
    longest = result.shape.index(max(result.shape))
    spots = []
    for shift in (0, 1):
        where = [jax.random.randint(jax.random.fold_in(own_key, axis), (), 0, length) for axis, length in enumerate(result.shape)]
        where[longest] = (where[longest] + shift) % result.shape[longest]
        spots.append(tuple(where))
    return result.at[spots[0]].set(least).at[spots[1]].set(high)


def steps_of(stream_key, dims, pieces, low, top_value):
    def one(dim, shards_of):
        steps = jax.random.uniform(jax.random.fold_in(jax.random.fold_in(stream_key, 6), dim), (shards_of,), jnp.float32, low / len(pieces), top_value / len(pieces))
        return jnp.repeat(jnp.exp(steps), dims[dim] // shards_of).reshape((-1,) + (1,) * (len(dims) - dim - 1))

    factor_of = one(*pieces[0])
    for cut in pieces[1:]:
        factor_of = factor_of * one(*cut)
    return factor_of


def shared_out(rng, own, number, rows, number_of, top, most, slope):
    sequence = jax.random.permutation(rng, number_of)
    heavy_load, usual = shares(number_of, rows * top, most, slope, True), shares(number_of, rows * top, most, slope, False)
    places = jnp.arange(number_of)

    def named(lengths, offset_by):
        used = int((lengths > 0).sum())
        fixed = max(1, used // 4)
        shifted = fixed + (places - fixed + offset_by * (used - fixed)) % max(1, number_of - fixed)
        return jnp.zeros((number_of,), jnp.int32).at[sequence[jnp.where(places < fixed, places, shifted)]].set(jnp.asarray(lengths, jnp.int32))

    lengths = jnp.where(number % 4 == 0, named(heavy_load, number // 4), named(usual, number - number // 4 - 1))
    mixed = jax.random.permutation(jax.random.fold_in(own, 3), number_of)
    giver, sink = mixed[0:number_of // 2 * 2:2], mixed[1:number_of // 2 * 2:2]
    margin = jnp.minimum(lengths[giver] - 1, most - lengths[sink]) // 2
    margin = jnp.where((giver == sequence[0]) | (sink == sequence[0]) | (lengths[sink] == 0), 0, jnp.maximum(margin, 0))
    shifted = jax.random.randint(jax.random.fold_in(own, 4), (number_of // 2,), 0, 1 << 20) % (margin + 1)
    lengths = lengths.at[giver].add(-shifted).at[sink].add(shifted)
    labels = jnp.searchsorted(jnp.cumsum(lengths), jnp.arange(rows * top), side="right").astype(jnp.int32)
    table = labels.reshape(top, rows).T
    table = table[jax.random.permutation(jax.random.fold_in(own, 1), rows)]
    offset_by = jax.random.randint(jax.random.fold_in(own, 2), (rows, 1), 0, top)
    return jnp.take_along_axis(table, (jnp.arange(top)[None, :] + offset_by) % top, axis=1)


def shares(count, total, bound, skew, full):
    weights = [(1 << 20) // math.isqrt(standing ** skew) + 1 for standing in range(1, count + 1)]
    largest = bound if full else min(bound, max(-(-total // count), total * weights[0] // sum(weights)))
    least = 1 if total - largest >= count - 1 else 0
    counts, surplus = [largest] + [least] * (count - 1), total - largest - least * (count - 1)
    while surplus > 0:
        candidates = [i for i in range(1, count) if counts[i] < largest] or [i for i in range(1, count) if counts[i] < bound]
        mass, budget = sum([weights[i] for i in candidates]), surplus
        for i in candidates:
            addition = min(bound - counts[i], max(1, budget * weights[i] // mass), surplus)
            counts[i] = counts[i] + addition
            surplus = surplus - addition
    return np.array(counts)


def scatter_about(rng, shape, width, bound, shards=(), dtype=jnp.bfloat16):
    result = width * jax.random.normal(rng, shape, jnp.float32)
    if shards:
        result = result * steps_of(rng, shape, shards, -0.22, 0.18)
    return jnp.clip(result, -bound, bound).astype(dtype)


def setup_inputs(seed: int = 0) -> dict:
    seeds = jax.random.split(jax.random.key(seed), 9)
    tokens = scatter_about(seeds[0], (ROWS, MODEL_WIDTH), 1.0, 6.0, ((0, 128),))
    holder_keys = jax.random.split(jax.random.fold_in(seeds[1], 1), ROWS // TOK_DEV)
    holder_turns = jax.random.permutation(jax.random.fold_in(seeds[1], 3), ROWS // TOK_DEV)
    holder = jax.vmap(lambda own, number: shared_out(jax.random.fold_in(seeds[1], 2), own, number, TOK_DEV, N_GRP * N_TP, 1, CAP, 2))(holder_keys, holder_turns).reshape((ROWS, 1))
    adapter_choice_index = set_ends(jax.random.randint(seeds[2], (ROWS, 1), 0, TEN_DEV), jax.random.fold_in(seeds[2], 1), 0, TEN_DEV - 1).astype(jnp.int32)
    query_base_output = scatter_about(seeds[3], (MODEL_WIDTH, DQ), MODEL_WIDTH ** -0.5, 0.0625, ((1, 16),))
    value_base_output = scatter_about(seeds[4], (MODEL_WIDTH, DV), MODEL_WIDTH ** -0.5, 0.0625, ((1, 16),))
    adapter_down_weight = scatter_about(seeds[5], (ADAPTER_TOTAL, MODEL_WIDTH, 2 * ADAPTER_RANK), MODEL_WIDTH ** -0.5, 0.0625, ((0, 128),))
    adapter_query_up = scatter_about(seeds[6], (ADAPTER_TOTAL, ADAPTER_RANK, DQ), ADAPTER_RANK ** -0.5, 0.75, ((0, 128),))
    adapter_value_up = scatter_about(seeds[7], (ADAPTER_TOTAL, ADAPTER_RANK, DV), ADAPTER_RANK ** -0.5, 0.75, ((0, 128),))
    return dict(tokens=tokens, holder=holder, adapter_choice_index=adapter_choice_index, query_base_output=query_base_output, value_base_output=value_base_output, adapter_down_weight=adapter_down_weight, adapter_query_up=adapter_query_up, adapter_value_up=adapter_value_up)


adapter_scale = 2.0


def reference(tokens, holder, adapter_choice_index, query_base_output, value_base_output, adapter_down_weight, adapter_query_up, adapter_value_up):
    tenant = (holder[:, 0] * TEN_DEV + adapter_choice_index[:, 0]).astype(jnp.int32)
    plain_query = jnp.dot(tokens, query_base_output, preferred_element_type=jnp.float32).astype(jnp.bfloat16)
    plain_value = jnp.dot(tokens, value_base_output, preferred_element_type=jnp.float32).astype(jnp.bfloat16)
    block_rows = 8
    row_blocks = tokens.reshape(ROWS // block_rows, block_rows, MODEL_WIDTH)
    tenant_blocks = tenant.reshape(ROWS // block_rows, block_rows)

    def one_block(pair):
        rows, adapter_index = pair
        down_weight = adapter_down_weight[adapter_index].astype(jnp.float32)
        reduced_state = jnp.einsum("bd,bdk->bk", rows.astype(jnp.float32), down_weight).astype(jnp.bfloat16)
        query_up_weight = adapter_query_up[adapter_index].astype(jnp.float32)
        value_up_weight = adapter_value_up[adapter_index].astype(jnp.float32)
        query_correction = (adapter_scale * jnp.einsum("jt,jtd->jd", reduced_state[:, :ADAPTER_RANK].astype(jnp.float32), query_up_weight)).astype(jnp.bfloat16)
        value_correction = (adapter_scale * jnp.einsum("jt,jtd->jd", reduced_state[:, ADAPTER_RANK:].astype(jnp.float32), value_up_weight)).astype(jnp.bfloat16)
        return query_correction, value_correction

    query_correction, value_correction = lax.map(one_block, (row_blocks, tenant_blocks))
    query_correction = query_correction.reshape(ROWS, DQ)
    value_correction = value_correction.reshape(ROWS, DV)
    queries = (plain_query.astype(jnp.float32) + query_correction.astype(jnp.float32)).astype(jnp.bfloat16)
    values = (plain_value.astype(jnp.float32) + value_correction.astype(jnp.float32)).astype(jnp.bfloat16)
    return queries, values
```

```python
import jax
import jax.numpy as jnp
from jax import lax
from jax.sharding import PartitionSpec as P

adapter_scale = 2.0
BF = jnp.bfloat16
F32 = jnp.float32
side = 4


def shift(x, dy, dz):
    pairs = [
        (y * side + z, (y + dy) % side * side + (z + dz) % side)
        for y in range(side)
        for z in range(side)
    ]
    return lax.ppermute(x, "tp", pairs)


def line_gather(x, step):
    back = (-step[0], -step[1])
    half = x.shape[0] // 2
    before = shift(x, *step)
    after = shift(x, *back)
    far_low = shift(before[:half], *step)
    far_high = shift(after[half:], *back)
    return after, (far_low, far_high), before


def to_absolute(blocks, place):
    for bit in (1, 2):
        moved = jnp.roll(blocks, bit, axis=0)
        blocks = jnp.where((place & bit) != 0, moved, blocks)
    return blocks


def apply_lowrank_adapters(rows, choice, adapter_down_weight, adapter_query_up, adapter_value_up):
    rank = adapter_query_up.shape[1]
    count = adapter_down_weight.shape[0]
    query_parts, value_parts = [], []
    for i in range(count):
        reduced = jnp.dot(rows, adapter_down_weight[i], preferred_element_type=F32)
        reduced = jnp.where(choice == i, reduced, 0.0).astype(BF)
        query_parts.append(reduced[:, :rank])
        value_parts.append(reduced[:, rank:])
    query_low = jnp.concatenate(query_parts, axis=1)
    value_low = jnp.concatenate(value_parts, axis=1)
    query_up = adapter_query_up.reshape(count * rank, adapter_query_up.shape[2])
    value_up = adapter_value_up.reshape(count * rank, adapter_value_up.shape[2])
    query = (adapter_scale * jnp.dot(query_low, query_up, preferred_element_type=F32)).astype(BF)
    value = (adapter_scale * jnp.dot(value_low, value_up, preferred_element_type=F32)).astype(BF)
    return query, value


def on_device(
    tokens,
    holder,
    adapter_choice_index,
    query_base_output,
    value_base_output,
    adapter_down_weight,
    adapter_query_up,
    adapter_value_up,
):
    row_count, width = tokens.shape
    query_cols = query_base_output.shape[1]
    value_cols = value_base_output.shape[1]
    both = query_cols + value_cols
    members = lax.axis_size("tp")
    devices = lax.axis_size("grp") * members
    capacity = 2
    slot_total = devices * capacity
    place = lax.axis_index("tp")

    holder_id = holder[:, 0]
    same_holder = holder_id[:, None] == holder_id[None, :]
    index = jnp.arange(row_count, dtype=jnp.int32)
    earlier = index[:, None] > index[None, :]
    position = jnp.sum((same_holder & earlier).astype(jnp.int32), axis=1)
    slot_index = holder_id * capacity + position
    pick_table = (jnp.arange(slot_total, dtype=jnp.int32)[:, None] == slot_index[None, :]).astype(BF)
    marked = jnp.concatenate(
        [tokens, jnp.broadcast_to(adapter_choice_index.astype(BF), (row_count, 128))], axis=1
    )
    send_rows = jnp.dot(pick_table, marked, preferred_element_type=F32).astype(BF)
    got_rows = lax.all_to_all(
        send_rows.reshape(devices, capacity, width + 128),
        ("grp", "tp"),
        split_axis=0,
        concat_axis=0,
        tiled=True,
    ).reshape(slot_total, width + 128)
    query_term, value_term = apply_lowrank_adapters(
        got_rows[:, :width],
        got_rows[:, width : width + 1],
        adapter_down_weight,
        adapter_query_up,
        adapter_value_up,
    )
    terms = jnp.concatenate([query_term, value_term], axis=1)
    back = lax.all_to_all(
        terms.reshape(devices, capacity, terms.shape[1]),
        ("grp", "tp"),
        split_axis=0,
        concat_axis=0,
        tiled=True,
    ).reshape(slot_total, terms.shape[1])
    half = width // 2
    along_z, along_y = (0, 1), (1, 0)
    weights = jnp.concatenate([query_base_output, value_base_output], axis=1)
    partial = []
    for part, first, second in ((0, along_z, along_y), (1, along_y, along_z)):
        own = tokens[:, part * half : (part + 1) * half]
        w = weights[part * half : (part + 1) * half]
        after, far, before = line_gather(own, first)
        line = jnp.concatenate([own, after, *far, before], axis=0)
        after, far, before = line_gather(line, second)
        far = jnp.concatenate(far, axis=0)
        partial.append(
            jnp.stack(
                [
                    jnp.dot(x, w, preferred_element_type=F32).reshape(side, row_count, both)
                    for x in (line, after, far, before)
                ]
            )
        )
    projected = (partial[0] + jnp.swapaxes(partial[1], 0, 1)).astype(BF)
    projected = to_absolute(projected, place // side)
    projected = jnp.swapaxes(to_absolute(jnp.swapaxes(projected, 0, 1), place % side), 0, 1)
    projected, back = lax.optimization_barrier((projected, back))
    row_terms = jnp.dot(pick_table.T, back, preferred_element_type=F32)
    plain = lax.all_to_all(
        projected.reshape(members, row_count, both), "tp", split_axis=0, concat_axis=0, tiled=True
    )
    plain = jnp.swapaxes(plain, 0, 1)
    plain_query = plain[:, :, :query_cols].reshape(row_count, members * query_cols)
    plain_value = plain[:, :, query_cols:].reshape(row_count, members * value_cols)
    split = plain_query.shape[1]
    queries = (plain_query.astype(F32) + row_terms[:, :split]).astype(BF)
    values = (plain_value.astype(F32) + row_terms[:, split:]).astype(BF)
    return (queries, values)


def solution(mesh):
    return jax.shard_map(
        on_device,
        mesh=mesh,
        in_specs=(
            P(("grp", "tp"), None),
            P(("grp", "tp"), None),
            P(("grp", "tp"), None),
            P(None, "tp"),
            P(None, "tp"),
            P(("grp", "tp"), None, None),
            P(("grp", "tp"), None, None),
            P(("grp", "tp"), None, None),
        ),
        out_specs=(P(("grp", "tp"), None), P(("grp", "tp"), None)),
        check_vma=False,
    )
```

```python
import jax
import jax.numpy as jnp
from jax import lax
from jax.experimental import pallas as pl
from jax.experimental.pallas import tpu as pltpu
from jax.sharding import PartitionSpec as P

adapter_scale = 2.0
BF = jnp.bfloat16
F32 = jnp.float32
side = 4


def shift(x, dy, dz):
    pairs = [
        (y * side + z, (y + dy) % side * side + (z + dz) % side)
        for y in range(side)
        for z in range(side)
    ]
    return lax.ppermute(x, "tp", pairs)


def line_gather(x, step):
    back = (-step[0], -step[1])
    half = x.shape[0] // 2
    before = shift(x, *step)
    after = shift(x, *back)
    far_low = shift(before[:half], *step)
    far_high = shift(after[half:], *back)
    return after, (far_low, far_high), before


def to_absolute(blocks, place):
    for bit in (1, 2):
        moved = jnp.roll(blocks, bit, axis=0)
        blocks = jnp.where((place & bit) != 0, moved, blocks)
    return blocks


def apply_lowrank_adapters(rows, choice, adapter_down_weight, adapter_query_up, adapter_value_up):
    rank = adapter_query_up.shape[1]
    count = adapter_down_weight.shape[0]
    query_parts, value_parts = [], []
    for i in range(count):
        reduced = jnp.dot(rows, adapter_down_weight[i], preferred_element_type=F32)
        reduced = jnp.where(choice == i, reduced, 0.0).astype(BF)
        query_parts.append(reduced[:, :rank])
        value_parts.append(reduced[:, rank:])
    query_low = jnp.concatenate(query_parts, axis=1)
    value_low = jnp.concatenate(value_parts, axis=1)
    query_up = adapter_query_up.reshape(count * rank, adapter_query_up.shape[2])
    value_up = adapter_value_up.reshape(count * rank, adapter_value_up.shape[2])
    query = (adapter_scale * jnp.dot(query_low, query_up, preferred_element_type=F32)).astype(BF)
    value = (adapter_scale * jnp.dot(value_low, value_up, preferred_element_type=F32)).astype(BF)
    return query, value


def finish_kernel(slot_ref, plain_ref, query_ref, value_ref, queries_ref, values_ref):
    rows, query_cols = plain_ref.shape[1], queries_ref.shape[1] // 2
    slots = query_ref.shape[0]
    pick = (lax.broadcasted_iota(jnp.int32, (rows, slots), 1) == slot_ref[...]).astype(BF)
    term = jnp.dot(pick, query_ref[...], preferred_element_type=F32)
    for i in range(2):
        cols = pl.ds(i * query_cols, query_cols)
        base = plain_ref[i, :, :query_cols].astype(F32)
        queries_ref[:, cols] = (base + term[:, i * query_cols : (i + 1) * query_cols]).astype(BF)
    term = jnp.dot(pick, value_ref[...], preferred_element_type=F32)
    base = jnp.concatenate([plain_ref[0, :, query_cols:], plain_ref[1, :, query_cols:]], axis=1)
    values_ref[...] = (base.astype(F32) + term).astype(BF)


def finish(slot_index, plain, terms, query_cols, value_cols):
    members, rows, both = plain.shape
    slots = terms.shape[0]
    value_at = members * query_cols // (2 * value_cols)
    return pl.pallas_call(
        finish_kernel,
        grid=(members // 2,),
        in_specs=[
            pl.BlockSpec((rows, 1), lambda i: (0, 0)),
            pl.BlockSpec((2, rows, both), lambda i: (i, 0, 0)),
            pl.BlockSpec((slots, 2 * query_cols), lambda i: (0, i)),
            pl.BlockSpec((slots, 2 * value_cols), lambda i: (0, value_at + i)),
        ],
        out_specs=[
            pl.BlockSpec((rows, 2 * query_cols), lambda i: (0, i)),
            pl.BlockSpec((rows, 2 * value_cols), lambda i: (0, i)),
        ],
        out_shape=[
            jax.ShapeDtypeStruct((rows, members * query_cols), BF),
            jax.ShapeDtypeStruct((rows, members * value_cols), BF),
        ],
        compiler_params=pltpu.CompilerParams(vmem_limit_bytes=24 << 20),
        cost_estimate=pl.CostEstimate(
            flops=2 * rows * slots * members * (query_cols + value_cols),
            bytes_accessed=2 * (slots + 2 * rows) * members * (query_cols + value_cols),
            transcendentals=0,
        ),
    )(slot_index[:, None], plain, terms, terms)


def on_device(
    tokens,
    holder,
    adapter_choice_index,
    query_base_output,
    value_base_output,
    adapter_down_weight,
    adapter_query_up,
    adapter_value_up,
):
    row_count, width = tokens.shape
    query_cols = query_base_output.shape[1]
    value_cols = value_base_output.shape[1]
    both = query_cols + value_cols
    members = lax.axis_size("tp")
    devices = lax.axis_size("grp") * members
    capacity = 2
    slot_total = devices * capacity
    place = lax.axis_index("tp")

    holder_id = holder[:, 0]
    same_holder = holder_id[:, None] == holder_id[None, :]
    index = jnp.arange(row_count, dtype=jnp.int32)
    earlier = index[:, None] > index[None, :]
    position = jnp.sum((same_holder & earlier).astype(jnp.int32), axis=1)
    slot_index = holder_id * capacity + position
    pick_table = (jnp.arange(slot_total, dtype=jnp.int32)[:, None] == slot_index[None, :]).astype(BF)
    marked = jnp.concatenate(
        [tokens, jnp.broadcast_to(adapter_choice_index.astype(BF), (row_count, 128))], axis=1
    )
    send_rows = jnp.dot(pick_table, marked, preferred_element_type=F32).astype(BF)
    send_rows = send_rows.reshape(devices, capacity, width + 128)

    half = width // 2
    along_z, along_y = (0, 1), (1, 0)
    weights = jnp.concatenate([query_base_output, value_base_output], axis=1)
    lines = []
    for part, step in ((0, along_z), (1, along_y)):
        own = tokens[:, part * half : (part + 1) * half]
        after, far, before = line_gather(own, step)
        lines.append(jnp.concatenate([own, after, *far, before], axis=0))
    lines[0], lines[1], send_rows = lax.optimization_barrier((lines[0], lines[1], send_rows))
    got_rows = lax.all_to_all(
        send_rows, ("grp", "tp"), split_axis=0, concat_axis=0, tiled=True
    ).reshape(slot_total, width + 128)
    query_term, value_term = apply_lowrank_adapters(
        got_rows[:, :width],
        got_rows[:, width : width + 1],
        adapter_down_weight,
        adapter_query_up,
        adapter_value_up,
    )
    terms = jnp.concatenate([query_term, value_term], axis=1)
    back = lax.all_to_all(
        terms.reshape(devices, capacity, terms.shape[1]),
        ("grp", "tp"),
        split_axis=0,
        concat_axis=0,
        tiled=True,
    ).reshape(slot_total, terms.shape[1])

    gathered = []
    for line, step in zip(lines, (along_y, along_z)):
        after, far, before = line_gather(line, step)
        gathered.append([line, after, jnp.concatenate(far, axis=0), before])
    gathered[1][3], back = lax.optimization_barrier((gathered[1][3], back))
    partial = []
    for part in range(2):
        w = weights[part * half : (part + 1) * half]
        partial.append(
            jnp.stack(
                [
                    jnp.dot(x, w, preferred_element_type=F32).reshape(side, row_count, both)
                    for x in gathered[part]
                ]
            )
        )
    projected = (partial[0] + jnp.swapaxes(partial[1], 0, 1)).astype(BF)
    projected = to_absolute(projected, place // side)
    projected = jnp.swapaxes(to_absolute(jnp.swapaxes(projected, 0, 1), place % side), 0, 1)
    plain = lax.all_to_all(
        projected.reshape(members, row_count, both), "tp", split_axis=0, concat_axis=0, tiled=True
    )
    queries, values = finish(slot_index, plain, back, query_cols, value_cols)
    return (queries, values)


def solution(mesh):
    return jax.shard_map(
        on_device,
        mesh=mesh,
        in_specs=(
            P(("grp", "tp"), None),
            P(("grp", "tp"), None),
            P(("grp", "tp"), None),
            P(None, "tp"),
            P(None, "tp"),
            P(("grp", "tp"), None, None),
            P(("grp", "tp"), None, None),
            P(("grp", "tp"), None, None),
        ),
        out_specs=(P(("grp", "tp"), None), P(("grp", "tp"), None)),
        check_vma=False,
    )
```

```python
import jax
import jax.numpy as jnp
from jax import lax
from jax.experimental import pallas as pl
from jax.experimental.pallas import tpu as pltpu
from jax.sharding import PartitionSpec as P

adapter_scale = 2.0
BF = jnp.bfloat16
F32 = jnp.float32
side = 4


def shift(x, dy, dz):
    pairs = [
        (y * side + z, (y + dy) % side * side + (z + dz) % side)
        for y in range(side)
        for z in range(side)
    ]
    return lax.ppermute(x, "tp", pairs)


def line_sides(x, step):
    return shift(x, -step[0], -step[1]), shift(x, *step)


def line_far(after, before, step):
    half = before.shape[0] // 2
    return shift(before[:half], *step), shift(after[half:], -step[0], -step[1])


def line_gather(x, step):
    after, before = line_sides(x, step)
    return after, line_far(after, before, step), before


def to_absolute(blocks, place):
    for bit in (1, 2):
        moved = jnp.roll(blocks, bit, axis=0)
        blocks = jnp.where((place & bit) != 0, moved, blocks)
    return blocks


def apply_lowrank_adapters(rows, choice, adapter_down_weight, adapter_query_up, adapter_value_up):
    rank = adapter_query_up.shape[1]
    count = adapter_down_weight.shape[0]
    query_parts, value_parts = [], []
    for i in range(count):
        reduced = jnp.dot(rows, adapter_down_weight[i], preferred_element_type=F32)
        reduced = jnp.where(choice == i, reduced, 0.0).astype(BF)
        query_parts.append(reduced[:, :rank])
        value_parts.append(reduced[:, rank:])
    query_low = jnp.concatenate(query_parts, axis=1)
    value_low = jnp.concatenate(value_parts, axis=1)
    query_up = adapter_query_up.reshape(count * rank, adapter_query_up.shape[2])
    value_up = adapter_value_up.reshape(count * rank, adapter_value_up.shape[2])
    query = (adapter_scale * jnp.dot(query_low, query_up, preferred_element_type=F32)).astype(BF)
    value = (adapter_scale * jnp.dot(value_low, value_up, preferred_element_type=F32)).astype(BF)
    return query, value


def finish_kernel(plain_ref, query_term_ref, value_term_ref, queries_ref, values_ref):
    query_cols = queries_ref.shape[1] // 2
    for i in range(2):
        cols = slice(i * query_cols, (i + 1) * query_cols)
        base = plain_ref[i, :, :query_cols].astype(F32)
        queries_ref[:, cols] = (base + query_term_ref[:, cols].astype(F32)).astype(BF)
    base = jnp.concatenate([plain_ref[0, :, query_cols:], plain_ref[1, :, query_cols:]], axis=1)
    values_ref[...] = (base.astype(F32) + value_term_ref[...].astype(F32)).astype(BF)


def finish(plain, terms, query_cols, value_cols):
    members, rows, both = plain.shape
    value_at = members * query_cols // (2 * value_cols)
    return pl.pallas_call(
        finish_kernel,
        grid=(members // 2,),
        in_specs=[
            pl.BlockSpec((2, rows, both), lambda i: (i, 0, 0)),
            pl.BlockSpec((rows, 2 * query_cols), lambda i: (0, i)),
            pl.BlockSpec((rows, 2 * value_cols), lambda i: (0, value_at + i)),
        ],
        out_specs=[
            pl.BlockSpec((rows, 2 * query_cols), lambda i: (0, i)),
            pl.BlockSpec((rows, 2 * value_cols), lambda i: (0, i)),
        ],
        out_shape=[
            jax.ShapeDtypeStruct((rows, members * query_cols), BF),
            jax.ShapeDtypeStruct((rows, members * value_cols), BF),
        ],
        compiler_params=pltpu.CompilerParams(vmem_limit_bytes=24 << 20),
        cost_estimate=pl.CostEstimate(
            flops=rows * members * both, bytes_accessed=6 * rows * members * both, transcendentals=0
        ),
    )(plain, terms, terms)


def on_device(
    tokens,
    holder,
    adapter_choice_index,
    query_base_output,
    value_base_output,
    adapter_down_weight,
    adapter_query_up,
    adapter_value_up,
):
    row_count, width = tokens.shape
    query_cols = query_base_output.shape[1]
    value_cols = value_base_output.shape[1]
    both = query_cols + value_cols
    members = lax.axis_size("tp")
    devices = lax.axis_size("grp") * members
    capacity = 2
    slot_total = devices * capacity

    holder_id = holder[:, 0]
    same_holder = holder_id[:, None] == holder_id[None, :]
    index = jnp.arange(row_count, dtype=jnp.int32)
    earlier = index[:, None] > index[None, :]
    position = jnp.sum((same_holder & earlier).astype(jnp.int32), axis=1)
    slot_index = holder_id * capacity + position
    pick_table = (jnp.arange(slot_total, dtype=jnp.int32)[:, None] == slot_index[None, :]).astype(BF)
    marked = jnp.concatenate(
        [tokens, jnp.broadcast_to(adapter_choice_index.astype(BF), (row_count, 128))], axis=1
    )
    send_rows = jnp.dot(pick_table, marked, preferred_element_type=F32).astype(BF)
    send_rows = send_rows.reshape(devices, capacity, width + 128)

    got_rows = lax.all_to_all(
        send_rows, ("grp", "tp"), split_axis=0, concat_axis=0, tiled=True
    ).reshape(slot_total, width + 128)
    query_term, value_term = apply_lowrank_adapters(
        got_rows[:, :width],
        got_rows[:, width : width + 1],
        adapter_down_weight,
        adapter_query_up,
        adapter_value_up,
    )
    terms = jnp.concatenate([query_term, value_term], axis=1)
    back = lax.all_to_all(
        terms.reshape(devices, capacity, terms.shape[1]),
        ("grp", "tp"),
        split_axis=0,
        concat_axis=0,
        tiled=True,
    )

    half = width // 2
    along_z, along_y = (0, 1), (1, 0)
    gathered = []
    for part, (one, two) in enumerate(((along_z, along_y), (along_y, along_z))):
        own = tokens[:, part * half : (part + 1) * half]
        after, far, before = line_gather(own, one)
        line = jnp.concatenate([own, after, *far, before], axis=0)
        after, before = line_sides(line, two)
        gathered.append([line, after, before])
    query_base_output, value_base_output, _ = lax.optimization_barrier(
        (query_base_output, value_base_output, far[0][:16, :128])
    )
    weights = jnp.concatenate([query_base_output, value_base_output], axis=1)
    for blocks, two in zip(gathered, (along_y, along_z)):
        blocks.insert(2, jnp.concatenate(line_far(blocks[1], blocks[2], two), axis=0))
    partial = []
    for part in range(2):
        w = weights[part * half : (part + 1) * half]
        partial.append(
            jnp.stack(
                [
                    jnp.dot(x, w, preferred_element_type=F32).reshape(side, row_count, both)
                    for x in gathered[part]
                ]
            )
        )
    place = lax.axis_index("tp")
    projected = (partial[0] + jnp.swapaxes(partial[1], 0, 1)).astype(BF)
    projected = to_absolute(projected, place // side)
    projected = jnp.swapaxes(to_absolute(jnp.swapaxes(projected, 0, 1), place % side), 0, 1)
    projected, back = lax.optimization_barrier((projected, back))
    back = back.reshape(slot_total, back.shape[2])
    row_terms = jnp.dot(pick_table.T, back, preferred_element_type=F32).astype(BF)
    plain = lax.all_to_all(
        projected.reshape(members, row_count, both), "tp", split_axis=0, concat_axis=0, tiled=True
    )
    queries, values = finish(plain, row_terms, query_cols, value_cols)
    return (queries, values)


def solution(mesh):
    return jax.shard_map(
        on_device,
        mesh=mesh,
        in_specs=(
            P(("grp", "tp"), None),
            P(("grp", "tp"), None),
            P(("grp", "tp"), None),
            P(None, "tp"),
            P(None, "tp"),
            P(("grp", "tp"), None, None),
            P(("grp", "tp"), None, None),
            P(("grp", "tp"), None, None),
        ),
        out_specs=(P(("grp", "tp"), None), P(("grp", "tp"), None)),
        check_vma=False,
    )
```

```python
import jax
import jax.numpy as jnp
from jax import lax
from jax.experimental import pallas as pl
from jax.experimental.pallas import tpu as pltpu
from jax.sharding import PartitionSpec as P

adapter_scale = 2.0
BF = jnp.bfloat16
F32 = jnp.float32
side = 4


def shift(x, dy, dz):
    axis, by = ("y", dy) if dz == 0 else ("z", dz)
    return lax.ppermute(x, axis, [(i, (i + by) % side) for i in range(side)])


def line_sides(x, step):
    return shift(x, -step[0], -step[1]), shift(x, *step)


def line_far(after, before, step):
    half = before.shape[0] // 2
    return shift(before[:half], *step), shift(after[half:], -step[0], -step[1])


def line_gather(x, step):
    after, before = line_sides(x, step)
    return after, line_far(after, before, step), before


def to_offsets(blocks, place):
    for bit in (1, 2):
        moved = jnp.roll(blocks, -bit, axis=0)
        blocks = jnp.where((place & bit) != 0, moved, blocks)
    return blocks


def to_absolute(blocks, place):
    for bit in (1, 2):
        moved = jnp.roll(blocks, bit, axis=0)
        blocks = jnp.where((place & bit) != 0, moved, blocks)
    return blocks


def apply_lowrank_adapters(halves, choice, adapter_down_weight, adapter_query_up, adapter_value_up):
    rank = adapter_query_up.shape[1]
    count = adapter_down_weight.shape[0]
    half = halves[0].shape[1]
    query_parts, value_parts = [], []
    for i in range(count):
        down = adapter_down_weight[i]
        reduced = jnp.dot(halves[0], down[:half], preferred_element_type=F32)
        other = jnp.dot(halves[1], down[half:], preferred_element_type=F32)
        other = other.reshape(-1, side, side, 2, other.shape[1])
        reduced = reduced + jnp.swapaxes(other, 1, 2).reshape(reduced.shape)
        reduced = jnp.where(choice == i, reduced, 0.0).astype(BF)
        query_parts.append(reduced[:, :rank])
        value_parts.append(reduced[:, rank:])
    query_low = jnp.concatenate(query_parts, axis=1)
    value_low = jnp.concatenate(value_parts, axis=1)
    query_up = adapter_query_up.reshape(count * rank, adapter_query_up.shape[2])
    value_up = adapter_value_up.reshape(count * rank, adapter_value_up.shape[2])
    query = (adapter_scale * jnp.dot(query_low, query_up, preferred_element_type=F32)).astype(BF)
    value = (adapter_scale * jnp.dot(value_low, value_up, preferred_element_type=F32)).astype(BF)
    return query, value


def finish_kernel(plain_ref, query_term_ref, value_term_ref, queries_ref, values_ref):
    query_cols = queries_ref.shape[1] // 2
    for i in range(2):
        cols = slice(i * query_cols, (i + 1) * query_cols)
        base = plain_ref[i, :, :query_cols].astype(F32)
        queries_ref[:, cols] = (base + query_term_ref[:, cols].astype(F32)).astype(BF)
    base = jnp.concatenate([plain_ref[0, :, query_cols:], plain_ref[1, :, query_cols:]], axis=1)
    values_ref[...] = (base.astype(F32) + value_term_ref[...].astype(F32)).astype(BF)


def finish(plain, terms, query_cols, value_cols):
    members, rows, both = plain.shape
    value_at = members * query_cols // (2 * value_cols)
    return pl.pallas_call(
        finish_kernel,
        grid=(members // 2,),
        in_specs=[
            pl.BlockSpec((2, rows, both), lambda i: (i, 0, 0)),
            pl.BlockSpec((rows, 2 * query_cols), lambda i: (0, i)),
            pl.BlockSpec((rows, 2 * value_cols), lambda i: (0, value_at + i)),
        ],
        out_specs=[
            pl.BlockSpec((rows, 2 * query_cols), lambda i: (0, i)),
            pl.BlockSpec((rows, 2 * value_cols), lambda i: (0, i)),
        ],
        out_shape=[
            jax.ShapeDtypeStruct((rows, members * query_cols), BF),
            jax.ShapeDtypeStruct((rows, members * value_cols), BF),
        ],
        compiler_params=pltpu.CompilerParams(vmem_limit_bytes=24 << 20),
        cost_estimate=pl.CostEstimate(
            flops=rows * members * both, bytes_accessed=6 * rows * members * both, transcendentals=0
        ),
    )(plain, terms, terms)


def on_device(
    tokens,
    holder,
    adapter_choice_index,
    query_base_output,
    value_base_output,
    adapter_down_weight,
    adapter_query_up,
    adapter_value_up,
):
    row_count, width = tokens.shape
    query_cols = query_base_output.shape[1]
    value_cols = value_base_output.shape[1]
    both = query_cols + value_cols
    members = side * side
    devices = lax.axis_size("grp") * members
    capacity = 2
    slot_total = devices * capacity

    holder_id = holder[:, 0]
    same_holder = holder_id[:, None] == holder_id[None, :]
    index = jnp.arange(row_count, dtype=jnp.int32)
    earlier = index[:, None] > index[None, :]
    position = jnp.sum((same_holder & earlier).astype(jnp.int32), axis=1)
    slot_index = holder_id * capacity + position
    pick_table = (slot_index[:, None] == jnp.arange(slot_total, dtype=jnp.int32)[None, :]).astype(BF)
    at_y, at_z = lax.axis_index("y"), lax.axis_index("z")
    codes = jnp.stack([slot_index, adapter_choice_index[:, 0]])[None]
    codes = lax.all_gather(codes, ("y", "z"), axis=0, tiled=True).reshape(side, side, 2, row_count)

    half = width // 2
    along_z, along_y = (0, 1), (1, 0)
    gathered, halves = [], []
    for part, (one, two) in enumerate(((along_z, along_y), (along_y, along_z))):
        own = tokens[:, part * half : (part + 1) * half]
        after, far, before = line_gather(own, one)
        line = jnp.concatenate([own, after, *far, before], axis=0)
        after, before = line_sides(line, two)
        far = jnp.concatenate(line_far(after, before, two), axis=0)
        gathered.append([line, after, far, before])

        if part == 0:
            here, line_codes = at_z, lax.dynamic_index_in_dim(codes, at_y, 0, keepdims=False)
        else:
            here, line_codes = at_y, lax.dynamic_index_in_dim(codes, at_z, 1, keepdims=False)
        source = (here + jnp.arange(side, dtype=jnp.int32)) % side
        line_codes = to_offsets(line_codes, here)
        slot, choice = line_codes[:, 0], line_codes[:, 1]
        target = slot // capacity
        if part == 0:
            mine, across = target % side == here, target // side
        else:
            mine = target // side % side == here
            across = target // members * side + target % side
        to = (across * side + source[:, None]) * capacity + slot % capacity
        to = jnp.where(mine, to, -1).reshape(1, side * row_count)
        pick = (jnp.arange(slot_total, dtype=jnp.int32)[:, None] == to).astype(BF)
        rows = jnp.dot(pick, line, preferred_element_type=F32).astype(BF)
        if part == 0:
            marks = jnp.where(
                pick != 0, choice.reshape(1, side * row_count).astype(F32), 0.0
            ).sum(axis=1, keepdims=True)
            marks = jnp.broadcast_to(marks.astype(BF), (slot_total, 128))
            rows = jnp.concatenate([rows, marks], axis=1)
        rows = lax.all_to_all(
            rows.reshape(slot_total // 8, 8, rows.shape[1]),
            ("grp", "y") if part == 0 else ("grp", "z"),
            split_axis=0,
            concat_axis=0,
            tiled=True,
        )
        halves.append(rows.reshape(slot_total, rows.shape[2]))
    choice = halves[0][:, half : half + 1]
    halves[0] = halves[0][:, :half]
    query_term, value_term = apply_lowrank_adapters(
        halves, choice, adapter_down_weight, adapter_query_up, adapter_value_up
    )
    terms = jnp.concatenate([query_term, value_term], axis=1)
    back = lax.all_to_all(
        terms.reshape(devices, capacity, terms.shape[1]),
        ("grp", "y", "z"),
        split_axis=0,
        concat_axis=0,
        tiled=True,
    )
    weights = jnp.concatenate([query_base_output, value_base_output], axis=1)
    partial = []
    for part in range(2):
        w = weights[part * half : (part + 1) * half]
        partial.append(
            jnp.stack(
                [
                    jnp.dot(x, w, preferred_element_type=F32).reshape(side, row_count, both)
                    for x in gathered[part]
                ]
            )
        )
    projected = (partial[0] + jnp.swapaxes(partial[1], 0, 1)).astype(BF)
    projected = to_absolute(projected, at_y)
    projected = jnp.swapaxes(to_absolute(jnp.swapaxes(projected, 0, 1), at_z), 0, 1)
    projected, back = lax.optimization_barrier((projected, back))
    back = back.reshape(slot_total, back.shape[2])
    row_terms = jnp.dot(pick_table, back, preferred_element_type=F32).astype(BF)
    plain = lax.all_to_all(
        projected.reshape(members, row_count, both), ("y", "z"), split_axis=0, concat_axis=0, tiled=True
    )
    queries, values = finish(plain, row_terms, query_cols, value_cols)
    return (queries, values)


def solution(mesh):
    grid = mesh.devices.reshape(mesh.devices.shape[0], side, side)
    rows = P(("grp", "y", "z"), None)
    adapters = P(("grp", "y", "z"), None, None)
    columns = P(None, ("y", "z"))
    return jax.shard_map(
        on_device,
        mesh=jax.sharding.Mesh(grid, ("grp", "y", "z")),
        in_specs=(rows, rows, rows, columns, columns, adapters, adapters, adapters),
        out_specs=(rows, rows),
        check_vma=False,
    )
```

```python
import jax
import jax.numpy as jnp
from jax import lax
from jax.experimental import pallas as pl
from jax.experimental.pallas import tpu as pltpu
from jax.sharding import PartitionSpec as P

adapter_scale = 2.0
BF = jnp.bfloat16
F32 = jnp.float32
side = 4


def shift(x, dy, dz):
    axis, by = ("y", dy) if dz == 0 else ("z", dz)
    return lax.ppermute(x, axis, [(i, (i + by) % side) for i in range(side)])


def line_sides(x, step):
    return shift(x, -step[0], -step[1]), shift(x, *step)


def line_far(after, before, step):
    half = before.shape[0] // 2
    return shift(before[:half], *step), shift(after[half:], -step[0], -step[1])


def line_gather(x, step):
    after, before = line_sides(x, step)
    return after, line_far(after, before, step), before


def to_absolute(blocks, place):
    for bit in (1, 2):
        moved = jnp.roll(blocks, bit, axis=0)
        blocks = jnp.where((place & bit) != 0, moved, blocks)
    return blocks


def apply_lowrank_adapters(halves, choice, adapter_down_weight, adapter_query_up, adapter_value_up):
    rank = adapter_query_up.shape[1]
    count = adapter_down_weight.shape[0]
    half = halves[0].shape[1]
    query_parts, value_parts = [], []
    downs = [adapter_down_weight[i] for i in range(count)]
    other = [jnp.dot(halves[1], d[half:], preferred_element_type=F32) for d in downs]
    other = lax.optimization_barrier(jnp.concatenate(other, axis=1))
    other = other.reshape(-1, side, side, 2, other.shape[1])
    other = jnp.swapaxes(other, 1, 2).reshape(-1, other.shape[4])
    for i, d in enumerate(downs):
        reduced = jnp.dot(halves[0], d[:half], preferred_element_type=F32)
        reduced = reduced + other[:, 2 * rank * i : 2 * rank * (i + 1)]
        reduced = jnp.where(choice == i, reduced, 0.0).astype(BF)
        query_parts.append(reduced[:, :rank])
        value_parts.append(reduced[:, rank:])
    query_low = jnp.concatenate(query_parts, axis=1)
    value_low = jnp.concatenate(value_parts, axis=1)
    query_up = adapter_query_up.reshape(count * rank, adapter_query_up.shape[2])
    value_up = adapter_value_up.reshape(count * rank, adapter_value_up.shape[2])
    query = (adapter_scale * jnp.dot(query_low, query_up, preferred_element_type=F32)).astype(BF)
    value = (adapter_scale * jnp.dot(value_low, value_up, preferred_element_type=F32)).astype(BF)
    return query, value


def finish_kernel(plain_ref, query_term_ref, value_term_ref, queries_ref, values_ref):
    query_cols = queries_ref.shape[1] // 2
    for i in range(2):
        cols = slice(i * query_cols, (i + 1) * query_cols)
        base = plain_ref[i, :, :query_cols].astype(F32)
        queries_ref[:, cols] = (base + query_term_ref[:, cols].astype(F32)).astype(BF)
    base = jnp.concatenate([plain_ref[0, :, query_cols:], plain_ref[1, :, query_cols:]], axis=1)
    values_ref[...] = (base.astype(F32) + value_term_ref[...].astype(F32)).astype(BF)


def finish(plain, terms, query_cols, value_cols):
    members, rows, both = plain.shape
    value_at = members * query_cols // (2 * value_cols)
    return pl.pallas_call(
        finish_kernel,
        grid=(members // 2,),
        in_specs=[
            pl.BlockSpec((2, rows, both), lambda i: (i, 0, 0)),
            pl.BlockSpec((rows, 2 * query_cols), lambda i: (0, i)),
            pl.BlockSpec((rows, 2 * value_cols), lambda i: (0, value_at + i)),
        ],
        out_specs=[
            pl.BlockSpec((rows, 2 * query_cols), lambda i: (0, i)),
            pl.BlockSpec((rows, 2 * value_cols), lambda i: (0, i)),
        ],
        out_shape=[
            jax.ShapeDtypeStruct((rows, members * query_cols), BF),
            jax.ShapeDtypeStruct((rows, members * value_cols), BF),
        ],
        compiler_params=pltpu.CompilerParams(vmem_limit_bytes=24 << 20),
        cost_estimate=pl.CostEstimate(
            flops=rows * members * both, bytes_accessed=6 * rows * members * both, transcendentals=0
        ),
    )(plain, terms, terms)


def on_device(
    tokens,
    holder,
    adapter_choice_index,
    query_base_output,
    value_base_output,
    adapter_down_weight,
    adapter_query_up,
    adapter_value_up,
):
    row_count, width = tokens.shape
    query_cols = query_base_output.shape[1]
    value_cols = value_base_output.shape[1]
    both = query_cols + value_cols
    members = side * side
    devices = lax.axis_size("grp") * members
    capacity = 2
    slot_total = devices * capacity

    holder_id = holder[:, 0]
    same_holder = holder_id[:, None] == holder_id[None, :]
    index = jnp.arange(row_count, dtype=jnp.int32)
    earlier = index[:, None] > index[None, :]
    position = jnp.sum((same_holder & earlier).astype(jnp.int32), axis=1)
    slot_index = holder_id * capacity + position
    pick_table = (slot_index[:, None] == jnp.arange(slot_total, dtype=jnp.int32)[None, :]).astype(BF)
    at_y, at_z = lax.axis_index("y"), lax.axis_index("z")
    codes = jnp.concatenate([slot_index[:, None], adapter_choice_index], axis=1).astype(BF)
    codes = jnp.pad(codes, ((0, 0), (0, 126)))

    half = width // 2
    along_z, along_y = (0, 1), (1, 0)
    gathered, halves = [], []
    for part, (one, two) in enumerate(((along_z, along_y), (along_y, along_z))):
        own = jnp.concatenate([tokens[:, part * half : (part + 1) * half], codes], axis=1)
        after, far, before = line_gather(own, one)
        pieces = (own, after, *far, before)
        line = jnp.concatenate([x[:, :half] for x in pieces], axis=0)
        line_codes = jnp.concatenate([x[:, half:] for x in pieces], axis=0)
        after, before = line_sides(line, two)
        gathered.append([line, after, before])

        here = at_z if part == 0 else at_y
        source = (here + jnp.arange(side * row_count, dtype=jnp.int32) // row_count) % side
        slot = line_codes[:, 0].astype(jnp.int32)
        target = slot // capacity
        if part == 0:
            mine, across = target % side == here, target // side
        else:
            mine = target // side % side == here
            across = target // members * side + target % side
        to = jnp.where(mine, (across * side + source) * capacity + slot % capacity, -1)
        pick = (jnp.arange(slot_total, dtype=jnp.int32)[:, None] == to[None, :]).astype(BF)
        rows = jnp.dot(pick, line, preferred_element_type=F32).astype(BF)
        if part == 0:
            marks = jnp.dot(pick, line_codes, preferred_element_type=F32).astype(BF)
            rows = jnp.concatenate([rows, marks], axis=1)
        rows = lax.all_to_all(
            rows.reshape(slot_total // 8, 8, rows.shape[1]),
            ("grp", "y") if part == 0 else ("grp", "z"),
            split_axis=0,
            concat_axis=0,
            tiled=True,
        )
        halves.append(rows.reshape(slot_total, rows.shape[2]))
    choice = halves[0][:, half + 1 : half + 2]
    halves[0] = halves[0][:, :half]
    query_term, value_term = apply_lowrank_adapters(
        halves, choice, adapter_down_weight, adapter_query_up, adapter_value_up
    )
    terms = jnp.concatenate([query_term, value_term], axis=1)
    terms = terms.reshape(devices, capacity, terms.shape[1])
    sides = [gathered[0][1], gathered[0][2], gathered[1][1], gathered[1][2]]
    sides, terms = lax.optimization_barrier((sides, terms))
    gathered[0][1:], gathered[1][1:] = sides[:2], sides[2:]
    for blocks, two in zip(gathered, (along_y, along_z)):
        blocks.insert(2, jnp.concatenate(line_far(blocks[1], blocks[2], two), axis=0))
    back = lax.all_to_all(terms, ("grp", "y", "z"), split_axis=0, concat_axis=0, tiled=True)
    weights = jnp.concatenate([query_base_output, value_base_output], axis=1)
    partial = []
    for part in range(2):
        w = weights[part * half : (part + 1) * half]
        partial.append(
            jnp.stack(
                [
                    jnp.dot(x, w, preferred_element_type=F32).reshape(side, row_count, both)
                    for x in gathered[part]
                ]
            )
        )
    projected = (partial[0] + jnp.swapaxes(partial[1], 0, 1)).astype(BF)
    projected = to_absolute(projected, at_y)
    projected = jnp.swapaxes(to_absolute(jnp.swapaxes(projected, 0, 1), at_z), 0, 1)
    projected, back = lax.optimization_barrier((projected, back))
    back = back.reshape(slot_total, back.shape[2])
    row_terms = jnp.dot(pick_table, back, preferred_element_type=F32).astype(BF)
    plain = lax.all_to_all(
        projected.reshape(members, row_count, both), ("y", "z"), split_axis=0, concat_axis=0, tiled=True
    )
    queries, values = finish(plain, row_terms, query_cols, value_cols)
    return (queries, values)


def solution(mesh):
    grid = mesh.devices.reshape(mesh.devices.shape[0], side, side)
    rows = P(("grp", "y", "z"), None)
    adapters = P(("grp", "y", "z"), None, None)
    columns = P(None, ("y", "z"))
    return jax.shard_map(
        on_device,
        mesh=jax.sharding.Mesh(grid, ("grp", "y", "z")),
        in_specs=(rows, rows, rows, columns, columns, adapters, adapters, adapters),
        out_specs=(rows, rows),
        check_vma=False,
    )
```

```python
import jax
import jax.numpy as jnp
from jax import lax
from jax.experimental import pallas as pl
from jax.experimental.pallas import tpu as pltpu
from jax.sharding import PartitionSpec as P

adapter_scale = 2.0
BF = jnp.bfloat16
F32 = jnp.float32
side = 4


def shift(x, dy, dz):
    pairs = [
        (y * side + z, (y + dy) % side * side + (z + dz) % side)
        for y in range(side)
        for z in range(side)
    ]
    return lax.ppermute(x, "tp", pairs)


def line_sides(x, step):
    return shift(x, -step[0], -step[1]), shift(x, *step)


def line_far(after, before, step):
    half = before.shape[0] // 2
    return shift(before[:half], *step), shift(after[half:], -step[0], -step[1])


def line_gather(x, step):
    after, before = line_sides(x, step)
    return after, line_far(after, before, step), before


def to_absolute(blocks, place):
    for bit in (1, 2):
        moved = jnp.roll(blocks, bit, axis=0)
        blocks = jnp.where((place & bit) != 0, moved, blocks)
    return blocks


def apply_lowrank_adapters(rows, choice, adapter_down_weight, adapter_query_up, adapter_value_up):
    rank = adapter_query_up.shape[1]
    count = adapter_down_weight.shape[0]
    query_parts, value_parts = [], []
    for i in range(count):
        reduced = jnp.dot(rows, adapter_down_weight[i], preferred_element_type=F32)
        reduced = jnp.where(choice == i, reduced, 0.0).astype(BF)
        query_parts.append(reduced[:, :rank])
        value_parts.append(reduced[:, rank:])
    query_low = jnp.concatenate(query_parts, axis=1)
    value_low = jnp.concatenate(value_parts, axis=1)
    query_up = adapter_query_up.reshape(count * rank, adapter_query_up.shape[2])
    value_up = adapter_value_up.reshape(count * rank, adapter_value_up.shape[2])
    query = (adapter_scale * jnp.dot(query_low, query_up, preferred_element_type=F32)).astype(BF)
    value = (adapter_scale * jnp.dot(value_low, value_up, preferred_element_type=F32)).astype(BF)
    return query, value


def finish_kernel(plain_ref, query_term_ref, value_term_ref, queries_ref, values_ref):
    query_cols = queries_ref.shape[1] // 2
    for i in range(2):
        cols = slice(i * query_cols, (i + 1) * query_cols)
        base = plain_ref[i, :, :query_cols].astype(F32)
        queries_ref[:, cols] = (base + query_term_ref[:, cols].astype(F32)).astype(BF)
    base = jnp.concatenate([plain_ref[0, :, query_cols:], plain_ref[1, :, query_cols:]], axis=1)
    values_ref[...] = (base.astype(F32) + value_term_ref[...].astype(F32)).astype(BF)


def finish(plain, terms, query_cols, value_cols):
    members, rows, both = plain.shape
    value_at = members * query_cols // (2 * value_cols)
    return pl.pallas_call(
        finish_kernel,
        grid=(members // 2,),
        in_specs=[
            pl.BlockSpec((2, rows, both), lambda i: (i, 0, 0)),
            pl.BlockSpec((rows, 2 * query_cols), lambda i: (0, i)),
            pl.BlockSpec((rows, 2 * value_cols), lambda i: (0, value_at + i)),
        ],
        out_specs=[
            pl.BlockSpec((rows, 2 * query_cols), lambda i: (0, i)),
            pl.BlockSpec((rows, 2 * value_cols), lambda i: (0, i)),
        ],
        out_shape=[
            jax.ShapeDtypeStruct((rows, members * query_cols), BF),
            jax.ShapeDtypeStruct((rows, members * value_cols), BF),
        ],
        compiler_params=pltpu.CompilerParams(vmem_limit_bytes=24 << 20),
        cost_estimate=pl.CostEstimate(
            flops=rows * members * both, bytes_accessed=6 * rows * members * both, transcendentals=0
        ),
    )(plain, terms, terms)


def on_device(
    tokens,
    holder,
    adapter_choice_index,
    query_base_output,
    value_base_output,
    adapter_down_weight,
    adapter_query_up,
    adapter_value_up,
):
    row_count, width = tokens.shape
    query_cols = query_base_output.shape[1]
    value_cols = value_base_output.shape[1]
    both = query_cols + value_cols
    members = lax.axis_size("tp")
    devices = lax.axis_size("grp") * members
    capacity = 2
    slot_total = devices * capacity

    holder_id = holder[:, 0]
    same_holder = holder_id[:, None] == holder_id[None, :]
    index = jnp.arange(row_count, dtype=jnp.int32)
    earlier = index[:, None] > index[None, :]
    position = jnp.sum((same_holder & earlier).astype(jnp.int32), axis=1)
    slot_index = holder_id * capacity + position
    pick_table = (jnp.arange(slot_total, dtype=jnp.int32)[:, None] == slot_index[None, :]).astype(BF)
    marked = jnp.concatenate(
        [tokens, jnp.broadcast_to(adapter_choice_index.astype(BF), (row_count, 128))], axis=1
    )
    send_rows = jnp.dot(pick_table, marked, preferred_element_type=F32).astype(BF)
    send_rows = send_rows.reshape(devices, capacity, width + 128)

    half = width // 2
    along_z, along_y = (0, 1), (1, 0)
    firsts = []
    for part, one in enumerate((along_z, along_y)):
        own = tokens[:, part * half : (part + 1) * half]
        after, far, before = line_gather(own, one)
        firsts.append((own, after, far, before))
    own, after, far, before = firsts[1]
    far, send_rows = lax.optimization_barrier((far, send_rows))
    firsts[1] = own, after, far, before
    got_rows = lax.all_to_all(
        send_rows, ("grp", "tp"), split_axis=0, concat_axis=0, tiled=True
    ).reshape(slot_total, width + 128)
    query_term, value_term = apply_lowrank_adapters(
        got_rows[:, :width],
        got_rows[:, width : width + 1],
        adapter_down_weight,
        adapter_query_up,
        adapter_value_up,
    )
    terms = jnp.concatenate([query_term, value_term], axis=1)
    terms = terms.reshape(devices, capacity, terms.shape[1])
    slot_index, terms = lax.optimization_barrier((slot_index, terms))
    back = lax.all_to_all(terms, ("grp", "tp"), split_axis=0, concat_axis=0, tiled=True)

    lines = [jnp.concatenate([own, after, *far, before], axis=0) for own, after, far, before in firsts]
    lines, query_base_output, value_base_output = lax.optimization_barrier(
        (lines, query_base_output, value_base_output)
    )
    weights = jnp.concatenate([query_base_output, value_base_output], axis=1)
    gathered = [[line, *line_sides(line, two)] for line, two in zip(lines, (along_y, along_z))]
    sides = [blocks[1:] for blocks in gathered]
    sides, slot_index = lax.optimization_barrier((sides, slot_index))
    for blocks, (after, before), two in zip(gathered, sides, (along_y, along_z)):
        far = jnp.concatenate(line_far(after, before, two), axis=0)
        blocks[1:] = [after, far, before]
    partial = []
    for part in range(2):
        w = weights[part * half : (part + 1) * half]
        partial.append(
            jnp.stack(
                [
                    jnp.dot(x, w, preferred_element_type=F32).reshape(side, row_count, both)
                    for x in gathered[part]
                ]
            )
        )
    place = lax.axis_index("tp")
    projected = (partial[0] + jnp.swapaxes(partial[1], 0, 1)).astype(BF)
    projected = to_absolute(projected, place // side)
    projected = jnp.swapaxes(to_absolute(jnp.swapaxes(projected, 0, 1), place % side), 0, 1)
    projected, back = lax.optimization_barrier((projected, back))
    back = back.reshape(slot_total, back.shape[2])
    pick_row = (slot_index[:, None] == jnp.arange(slot_total, dtype=jnp.int32)[None, :]).astype(BF)
    row_terms = jnp.dot(pick_row, back, preferred_element_type=F32).astype(BF)
    plain = lax.all_to_all(
        projected.reshape(members, row_count, both), "tp", split_axis=0, concat_axis=0, tiled=True
    )
    queries, values = finish(plain, row_terms, query_cols, value_cols)
    return (queries, values)


def solution(mesh):
    return jax.shard_map(
        on_device,
        mesh=mesh,
        in_specs=(
            P(("grp", "tp"), None),
            P(("grp", "tp"), None),
            P(("grp", "tp"), None),
            P(None, "tp"),
            P(None, "tp"),
            P(("grp", "tp"), None, None),
            P(("grp", "tp"), None, None),
            P(("grp", "tp"), None, None),
        ),
        out_specs=(P(("grp", "tp"), None), P(("grp", "tp"), None)),
        check_vma=False,
    )
```

```python
import jax
import jax.numpy as jnp
from jax import lax
from jax.experimental import pallas as pl
from jax.experimental.pallas import tpu as pltpu
from jax.sharding import PartitionSpec as P

adapter_scale = 2.0
BF = jnp.bfloat16
F32 = jnp.float32
side = 4


def shift(x, dy, dz):
    pairs = [
        (y * side + z, (y + dy) % side * side + (z + dz) % side)
        for y in range(side)
        for z in range(side)
    ]
    return lax.ppermute(x, "tp", pairs)


def line_sides(x, step):
    return shift(x, -step[0], -step[1]), shift(x, *step)


def line_far(after, before, step):
    half = before.shape[0] // 2
    return shift(before[:half], *step), shift(after[half:], -step[0], -step[1])


def line_gather(x, step):
    after, before = line_sides(x, step)
    return after, line_far(after, before, step), before


def to_absolute(blocks, place):
    for bit in (1, 2):
        moved = jnp.roll(blocks, bit, axis=0)
        blocks = jnp.where((place & bit) != 0, moved, blocks)
    return blocks


def apply_lowrank_adapters(rows, choice, adapter_down_weight, adapter_query_up, adapter_value_up):
    rank = adapter_query_up.shape[1]
    count = adapter_down_weight.shape[0]
    query_parts, value_parts = [], []
    for i in range(count):
        reduced = jnp.dot(rows, adapter_down_weight[i], preferred_element_type=F32)
        reduced = jnp.where(choice == i, reduced, 0.0).astype(BF)
        query_parts.append(reduced[:, :rank])
        value_parts.append(reduced[:, rank:])
    query_low = jnp.concatenate(query_parts, axis=1)
    value_low = jnp.concatenate(value_parts, axis=1)
    query_up = adapter_query_up.reshape(count * rank, adapter_query_up.shape[2])
    value_up = adapter_value_up.reshape(count * rank, adapter_value_up.shape[2])
    query = (adapter_scale * jnp.dot(query_low, query_up, preferred_element_type=F32)).astype(BF)
    value = (adapter_scale * jnp.dot(value_low, value_up, preferred_element_type=F32)).astype(BF)
    return query, value


def finish_kernel(plain_ref, query_term_ref, value_term_ref, queries_ref, values_ref):
    query_cols = queries_ref.shape[1] // 2
    for i in range(2):
        cols = slice(i * query_cols, (i + 1) * query_cols)
        base = plain_ref[i, :, :query_cols].astype(F32)
        queries_ref[:, cols] = (base + query_term_ref[:, cols].astype(F32)).astype(BF)
    base = jnp.concatenate([plain_ref[0, :, query_cols:], plain_ref[1, :, query_cols:]], axis=1)
    values_ref[...] = (base.astype(F32) + value_term_ref[...].astype(F32)).astype(BF)


def finish(plain, terms, query_cols, value_cols):
    members, rows, both = plain.shape
    value_at = members * query_cols // (2 * value_cols)
    return pl.pallas_call(
        finish_kernel,
        grid=(members // 2,),
        in_specs=[
            pl.BlockSpec((2, rows, both), lambda i: (i, 0, 0)),
            pl.BlockSpec((rows, 2 * query_cols), lambda i: (0, i)),
            pl.BlockSpec((rows, 2 * value_cols), lambda i: (0, value_at + i)),
        ],
        out_specs=[
            pl.BlockSpec((rows, 2 * query_cols), lambda i: (0, i)),
            pl.BlockSpec((rows, 2 * value_cols), lambda i: (0, i)),
        ],
        out_shape=[
            jax.ShapeDtypeStruct((rows, members * query_cols), BF),
            jax.ShapeDtypeStruct((rows, members * value_cols), BF),
        ],
        compiler_params=pltpu.CompilerParams(vmem_limit_bytes=24 << 20),
        cost_estimate=pl.CostEstimate(
            flops=rows * members * both, bytes_accessed=6 * rows * members * both, transcendentals=0
        ),
    )(plain, terms, terms)


def on_device(
    tokens,
    holder,
    adapter_choice_index,
    query_base_output,
    value_base_output,
    adapter_down_weight,
    adapter_query_up,
    adapter_value_up,
):
    row_count, width = tokens.shape
    query_cols = query_base_output.shape[1]
    value_cols = value_base_output.shape[1]
    both = query_cols + value_cols
    members = lax.axis_size("tp")
    devices = lax.axis_size("grp") * members
    capacity = 2
    slot_total = devices * capacity

    holder_id = holder[:, 0]
    same_holder = holder_id[:, None] == holder_id[None, :]
    index = jnp.arange(row_count, dtype=jnp.int32)
    earlier = index[:, None] > index[None, :]
    position = jnp.sum((same_holder & earlier).astype(jnp.int32), axis=1)
    slot_index = holder_id * capacity + position
    pick_table = (jnp.arange(slot_total, dtype=jnp.int32)[:, None] == slot_index[None, :]).astype(BF)
    marked = jnp.concatenate(
        [tokens, jnp.broadcast_to(adapter_choice_index.astype(BF), (row_count, 128))], axis=1
    )
    send_rows = jnp.dot(pick_table, marked, preferred_element_type=F32).astype(BF)
    send_rows = send_rows.reshape(devices, capacity, width + 128)

    half = width // 2
    along_z, along_y = (0, 1), (1, 0)
    firsts = []
    for part, one in enumerate((along_z, along_y)):
        own = tokens[:, part * half : (part + 1) * half]
        after, far, before = line_gather(own, one)
        firsts.append((own, after, far, before))
    own, after, far, before = firsts[1]
    far, send_rows = lax.optimization_barrier((far, send_rows))
    firsts[1] = own, after, far, before
    got_rows = lax.all_to_all(
        send_rows, ("grp", "tp"), split_axis=0, concat_axis=0, tiled=True
    ).reshape(slot_total, width + 128)
    query_term, value_term = apply_lowrank_adapters(
        got_rows[:, :width],
        got_rows[:, width : width + 1],
        adapter_down_weight,
        adapter_query_up,
        adapter_value_up,
    )
    terms = jnp.concatenate([query_term, value_term], axis=1)
    terms = terms.reshape(devices, capacity, terms.shape[1])
    slot_index, terms = lax.optimization_barrier((slot_index, terms))
    back = lax.all_to_all(terms, ("grp", "tp"), split_axis=0, concat_axis=0, tiled=True)

    lines = [jnp.concatenate([own, after, *far, before], axis=0) for own, after, far, before in firsts]
    lines, query_base_output, value_base_output = lax.optimization_barrier(
        (lines, query_base_output, value_base_output)
    )
    weights = jnp.concatenate([query_base_output, value_base_output], axis=1)
    gathered = [[line, *line_sides(line, two)] for line, two in zip(lines, (along_y, along_z))]
    sides = [blocks[1:] for blocks in gathered]
    sides = [list(x) for x in sides]
    fars = [
        jnp.concatenate(line_far(after, before, two), axis=0)
        for (after, before), two in zip(sides, (along_y, along_z))
    ]
    sides[1][1], back = lax.optimization_barrier((sides[1][1], back))
    for blocks, (after, before), far in zip(gathered, sides, fars):
        blocks[1:] = [after, far, before]
    partial = []
    for part in range(2):
        w = weights[part * half : (part + 1) * half]
        partial.append(
            jnp.stack(
                [
                    jnp.dot(x, w, preferred_element_type=F32).reshape(side, row_count, both)
                    for x in gathered[part]
                ]
            )
        )
    place = lax.axis_index("tp")
    projected = (partial[0] + jnp.swapaxes(partial[1], 0, 1)).astype(BF)
    projected = to_absolute(projected, place // side)
    projected = jnp.swapaxes(to_absolute(jnp.swapaxes(projected, 0, 1), place % side), 0, 1)
    projected, back = lax.optimization_barrier((projected, back))
    back = back.reshape(slot_total, back.shape[2])
    pick_row = (slot_index[:, None] == jnp.arange(slot_total, dtype=jnp.int32)[None, :]).astype(BF)
    row_terms = jnp.dot(pick_row, back, preferred_element_type=F32).astype(BF)
    plain = lax.all_to_all(
        projected.reshape(members, row_count, both), "tp", split_axis=0, concat_axis=0, tiled=True
    )
    queries, values = finish(plain, row_terms, query_cols, value_cols)
    return (queries, values)


def solution(mesh):
    return jax.shard_map(
        on_device,
        mesh=mesh,
        in_specs=(
            P(("grp", "tp"), None),
            P(("grp", "tp"), None),
            P(("grp", "tp"), None),
            P(None, "tp"),
            P(None, "tp"),
            P(("grp", "tp"), None, None),
            P(("grp", "tp"), None, None),
            P(("grp", "tp"), None, None),
        ),
        out_specs=(P(("grp", "tp"), None), P(("grp", "tp"), None)),
        check_vma=False,
    )
```

```python
import jax
import jax.numpy as jnp
from jax import lax
from jax.experimental import pallas as pl
from jax.experimental.pallas import tpu as pltpu
from jax.sharding import PartitionSpec as P

adapter_scale = 2.0
BF = jnp.bfloat16
F32 = jnp.float32
side = 4


def shift(x, dy, dz):
    pairs = [
        (y * side + z, (y + dy) % side * side + (z + dz) % side)
        for y in range(side)
        for z in range(side)
    ]
    return lax.ppermute(x, "tp", pairs)


def line_sides(x, step):
    return shift(x, -step[0], -step[1]), shift(x, *step)


def line_far(after, before, step):
    half = before.shape[0] // 2
    return shift(before[:half], *step), shift(after[half:], -step[0], -step[1])


def line_gather(x, step):
    after, before = line_sides(x, step)
    return after, line_far(after, before, step), before


def to_absolute(blocks, place):
    for bit in (1, 2):
        moved = jnp.roll(blocks, bit, axis=0)
        blocks = jnp.where((place & bit) != 0, moved, blocks)
    return blocks


def apply_lowrank_adapters(rows, choice, adapter_down_weight, adapter_query_up, adapter_value_up):
    rank = adapter_query_up.shape[1]
    count = adapter_down_weight.shape[0]
    query_parts, value_parts = [], []
    for i in range(count):
        reduced = jnp.dot(rows, adapter_down_weight[i], preferred_element_type=F32)
        reduced = jnp.where(choice == i, reduced, 0.0).astype(BF)
        query_parts.append(reduced[:, :rank])
        value_parts.append(reduced[:, rank:])
    query_low = jnp.concatenate(query_parts, axis=1)
    value_low = jnp.concatenate(value_parts, axis=1)
    query_up = adapter_query_up.reshape(count * rank, adapter_query_up.shape[2])
    value_up = adapter_value_up.reshape(count * rank, adapter_value_up.shape[2])
    query = (adapter_scale * jnp.dot(query_low, query_up, preferred_element_type=F32)).astype(BF)
    value = (adapter_scale * jnp.dot(value_low, value_up, preferred_element_type=F32)).astype(BF)
    return query, value


def finish_kernel(plain_ref, query_term_ref, value_term_ref, queries_ref, values_ref):
    query_cols = queries_ref.shape[1] // 2
    for i in range(2):
        cols = slice(i * query_cols, (i + 1) * query_cols)
        base = plain_ref[i, :, :query_cols].astype(F32)
        queries_ref[:, cols] = (base + query_term_ref[:, cols].astype(F32)).astype(BF)
    base = jnp.concatenate([plain_ref[0, :, query_cols:], plain_ref[1, :, query_cols:]], axis=1)
    values_ref[...] = (base.astype(F32) + value_term_ref[...].astype(F32)).astype(BF)


def finish(plain, terms, query_cols, value_cols):
    members, rows, both = plain.shape
    value_at = members * query_cols // (2 * value_cols)
    return pl.pallas_call(
        finish_kernel,
        grid=(members // 2,),
        in_specs=[
            pl.BlockSpec((2, rows, both), lambda i: (i, 0, 0)),
            pl.BlockSpec((rows, 2 * query_cols), lambda i: (0, i)),
            pl.BlockSpec((rows, 2 * value_cols), lambda i: (0, value_at + i)),
        ],
        out_specs=[
            pl.BlockSpec((rows, 2 * query_cols), lambda i: (0, i)),
            pl.BlockSpec((rows, 2 * value_cols), lambda i: (0, i)),
        ],
        out_shape=[
            jax.ShapeDtypeStruct((rows, members * query_cols), BF),
            jax.ShapeDtypeStruct((rows, members * value_cols), BF),
        ],
        compiler_params=pltpu.CompilerParams(vmem_limit_bytes=24 << 20),
        cost_estimate=pl.CostEstimate(
            flops=rows * members * both, bytes_accessed=6 * rows * members * both, transcendentals=0
        ),
    )(plain, terms, terms)


def on_device(
    tokens,
    holder,
    adapter_choice_index,
    query_base_output,
    value_base_output,
    adapter_down_weight,
    adapter_query_up,
    adapter_value_up,
):
    row_count, width = tokens.shape
    query_cols = query_base_output.shape[1]
    value_cols = value_base_output.shape[1]
    both = query_cols + value_cols
    members = lax.axis_size("tp")
    devices = lax.axis_size("grp") * members
    capacity = 2
    slot_total = devices * capacity

    holder_id = holder[:, 0]
    same_holder = holder_id[:, None] == holder_id[None, :]
    index = jnp.arange(row_count, dtype=jnp.int32)
    earlier = index[:, None] > index[None, :]
    position = jnp.sum((same_holder & earlier).astype(jnp.int32), axis=1)
    slot_index = holder_id * capacity + position
    pick_table = (jnp.arange(slot_total, dtype=jnp.int32)[:, None] == slot_index[None, :]).astype(BF)
    marked = jnp.concatenate(
        [tokens, jnp.broadcast_to(adapter_choice_index.astype(BF), (row_count, 128))], axis=1
    )
    send_rows = jnp.dot(pick_table, marked, preferred_element_type=F32).astype(BF)
    send_rows = send_rows.reshape(devices, capacity, width + 128)

    half = width // 2
    along_z, along_y = (0, 1), (1, 0)
    owns = [tokens[:, part * half : (part + 1) * half] for part in range(2)]
    nexts = [line_sides(own, one) for own, one in zip(owns, (along_z, along_y))]
    nexts, send_rows = lax.optimization_barrier((nexts, send_rows))
    firsts = [
        (own, after, line_far(after, before, one), before)
        for own, (after, before), one in zip(owns, nexts, (along_z, along_y))
    ]
    fars = [far for _, _, far, _ in firsts]
    fars, send_rows = lax.optimization_barrier((fars, send_rows))
    firsts = [(own, after, far, before) for (own, after, _, before), far in zip(firsts, fars)]
    got_rows = lax.all_to_all(
        send_rows, ("grp", "tp"), split_axis=0, concat_axis=0, tiled=True
    ).reshape(slot_total, width + 128)
    query_term, value_term = apply_lowrank_adapters(
        got_rows[:, :width],
        got_rows[:, width : width + 1],
        adapter_down_weight,
        adapter_query_up,
        adapter_value_up,
    )
    terms = jnp.concatenate([query_term, value_term], axis=1)
    terms = terms.reshape(devices, capacity, terms.shape[1])
    slot_index, terms = lax.optimization_barrier((slot_index, terms))
    back = lax.all_to_all(terms, ("grp", "tp"), split_axis=0, concat_axis=0, tiled=True)

    lines = [jnp.concatenate([own, after, *far, before], axis=0) for own, after, far, before in firsts]
    lines, query_base_output, value_base_output = lax.optimization_barrier(
        (lines, query_base_output, value_base_output)
    )
    weights = jnp.concatenate([query_base_output, value_base_output], axis=1)
    gathered = [[line, *line_sides(line, two)] for line, two in zip(lines, (along_y, along_z))]
    sides = [blocks[1:] for blocks in gathered]
    sides = [list(x) for x in sides]
    fars = [
        jnp.concatenate(line_far(after, before, two), axis=0)
        for (after, before), two in zip(sides, (along_y, along_z))
    ]
    for blocks, (after, before), far in zip(gathered, sides, fars):
        blocks[1:] = [after, far, before]
    cut = 3 * row_count
    last = gathered[1][3]
    gathered[1][3] = last[:cut]
    last, back = lax.optimization_barrier((last[cut:], back))
    partial = []
    for part in range(2):
        w = weights[part * half : (part + 1) * half]
        products = [jnp.dot(x, w, preferred_element_type=F32) for x in gathered[part]]
        if part == 1:
            extra = jnp.dot(last, w, preferred_element_type=F32)
            products[3] = jnp.concatenate([products[3], extra], axis=0)
        partial.append(jnp.stack([x.reshape(side, row_count, both) for x in products]))
    place = lax.axis_index("tp")
    projected = (partial[0] + jnp.swapaxes(partial[1], 0, 1)).astype(BF)
    projected = to_absolute(projected, place // side)
    projected = jnp.swapaxes(to_absolute(jnp.swapaxes(projected, 0, 1), place % side), 0, 1)
    projected, back = lax.optimization_barrier((projected, back))
    back = back.reshape(slot_total, back.shape[2])
    pick_row = (slot_index[:, None] == jnp.arange(slot_total, dtype=jnp.int32)[None, :]).astype(BF)
    row_terms = jnp.dot(pick_row, back, preferred_element_type=F32).astype(BF)
    plain = lax.all_to_all(
        projected.reshape(members, row_count, both), "tp", split_axis=0, concat_axis=0, tiled=True
    )
    queries, values = finish(plain, row_terms, query_cols, value_cols)
    return (queries, values)


def solution(mesh):
    return jax.shard_map(
        on_device,
        mesh=mesh,
        in_specs=(
            P(("grp", "tp"), None),
            P(("grp", "tp"), None),
            P(("grp", "tp"), None),
            P(None, "tp"),
            P(None, "tp"),
            P(("grp", "tp"), None, None),
            P(("grp", "tp"), None, None),
            P(("grp", "tp"), None, None),
        ),
        out_specs=(P(("grp", "tp"), None), P(("grp", "tp"), None)),
        check_vma=False,
    )
```

```python
import jax
import jax.numpy as jnp
from jax import lax
from jax.experimental import pallas as pl
from jax.experimental.pallas import tpu as pltpu
from jax.sharding import PartitionSpec as P

adapter_scale = 2.0
BF = jnp.bfloat16
F32 = jnp.float32
side = 4


def shift(x, dy, dz):
    pairs = [
        (y * side + z, (y + dy) % side * side + (z + dz) % side)
        for y in range(side)
        for z in range(side)
    ]
    return lax.ppermute(x, "tp", pairs)


def line_sides(x, step):
    return shift(x, -step[0], -step[1]), shift(x, *step)


def line_far(after, before, step):
    half = before.shape[0] // 2
    return shift(before[:half], *step), shift(after[half:], -step[0], -step[1])


def line_gather(x, step):
    after, before = line_sides(x, step)
    return after, line_far(after, before, step), before


def to_absolute(blocks, place):
    for bit in (1, 2):
        moved = jnp.roll(blocks, bit, axis=0)
        blocks = jnp.where((place & bit) != 0, moved, blocks)
    return blocks


def apply_lowrank_adapters(rows, choice, adapter_down_weight, adapter_query_up, adapter_value_up):
    rank = adapter_query_up.shape[1]
    count = adapter_down_weight.shape[0]
    query_parts, value_parts = [], []
    for i in range(count):
        reduced = jnp.dot(rows, adapter_down_weight[i], preferred_element_type=F32)
        reduced = jnp.where(choice == i, reduced, 0.0).astype(BF)
        query_parts.append(reduced[:, :rank])
        value_parts.append(reduced[:, rank:])
    query_low = jnp.concatenate(query_parts, axis=1)
    value_low = jnp.concatenate(value_parts, axis=1)
    query_up = adapter_query_up.reshape(count * rank, adapter_query_up.shape[2])
    value_up = adapter_value_up.reshape(count * rank, adapter_value_up.shape[2])
    query = (adapter_scale * jnp.dot(query_low, query_up, preferred_element_type=F32)).astype(BF)
    value = (adapter_scale * jnp.dot(value_low, value_up, preferred_element_type=F32)).astype(BF)
    return query, value


def finish_kernel(plain_ref, term_ref, queries_ref, values_ref):
    members, _, both = plain_ref.shape
    query_cols = queries_ref.shape[1] // members
    value_cols = both - query_cols
    for i in range(members):
        cols = slice(i * query_cols, (i + 1) * query_cols)
        base = plain_ref[i, :, :query_cols].astype(F32)
        queries_ref[:, cols] = (base + term_ref[:, cols].astype(F32)).astype(BF)
    at = members * query_cols
    for i in range(0, members, 2):
        base = jnp.concatenate([plain_ref[i, :, query_cols:], plain_ref[i + 1, :, query_cols:]], axis=1)
        cols = slice(i * value_cols, (i + 2) * value_cols)
        term = term_ref[:, at + i * value_cols : at + (i + 2) * value_cols].astype(F32)
        values_ref[:, cols] = (base.astype(F32) + term).astype(BF)


def finish(plain, terms, query_cols, value_cols):
    members, rows, both = plain.shape
    whole = pl.BlockSpec(memory_space=pltpu.VMEM)
    return pl.pallas_call(
        finish_kernel,
        in_specs=[whole, whole],
        out_specs=[whole, whole],
        out_shape=[
            jax.ShapeDtypeStruct((rows, members * query_cols), BF),
            jax.ShapeDtypeStruct((rows, members * value_cols), BF),
        ],
        compiler_params=pltpu.CompilerParams(vmem_limit_bytes=24 << 20),
        cost_estimate=pl.CostEstimate(
            flops=rows * members * both, bytes_accessed=6 * rows * members * both, transcendentals=0
        ),
    )(plain, terms)


def on_device(
    tokens,
    holder,
    adapter_choice_index,
    query_base_output,
    value_base_output,
    adapter_down_weight,
    adapter_query_up,
    adapter_value_up,
):
    row_count, width = tokens.shape
    query_cols = query_base_output.shape[1]
    value_cols = value_base_output.shape[1]
    both = query_cols + value_cols
    members = lax.axis_size("tp")
    devices = lax.axis_size("grp") * members
    capacity = 2
    slot_total = devices * capacity

    holder_id = holder[:, 0]
    same_holder = holder_id[:, None] == holder_id[None, :]
    index = jnp.arange(row_count, dtype=jnp.int32)
    earlier = index[:, None] > index[None, :]
    position = jnp.sum((same_holder & earlier).astype(jnp.int32), axis=1)
    slot_index = holder_id * capacity + position
    pick_table = (jnp.arange(slot_total, dtype=jnp.int32)[:, None] == slot_index[None, :]).astype(BF)
    marked = jnp.concatenate(
        [tokens, jnp.broadcast_to(adapter_choice_index.astype(BF), (row_count, 128))], axis=1
    )
    send_rows = jnp.dot(pick_table, marked, preferred_element_type=F32).astype(BF)
    send_rows = send_rows.reshape(devices, capacity, width + 128)

    got_rows = lax.all_to_all(
        send_rows, ("grp", "tp"), split_axis=0, concat_axis=0, tiled=True
    ).reshape(slot_total, width + 128)
    query_term, value_term = apply_lowrank_adapters(
        got_rows[:, :width],
        got_rows[:, width : width + 1],
        adapter_down_weight,
        adapter_query_up,
        adapter_value_up,
    )
    terms = jnp.concatenate([query_term, value_term], axis=1)
    back = lax.all_to_all(
        terms.reshape(devices, capacity, terms.shape[1]),
        ("grp", "tp"),
        split_axis=0,
        concat_axis=0,
        tiled=True,
    )

    half = width // 2
    along_z, along_y = (0, 1), (1, 0)
    gathered, line_blocks = [], []
    for part, (one, two) in enumerate(((along_z, along_y), (along_y, along_z))):
        own = tokens[:, part * half : (part + 1) * half]
        after, before = line_sides(own, one)
        low = jnp.concatenate([own, after], axis=0)
        line_blocks.append((low, *line_sides(low, two), after, before))
    sides = [blocks[1:3] for blocks in line_blocks]
    nexts = [blocks[3:] for blocks in line_blocks]
    sides, nexts = lax.optimization_barrier((sides, nexts))
    for (low, *_), (low_after, low_before), (after, before), (one, two) in zip(
        line_blocks, sides, nexts, ((along_z, along_y), (along_y, along_z))
    ):
        high = jnp.concatenate([*line_far(after, before, one), before], axis=0)
        high_after, high_before = line_sides(high, two)
        low_far, high_far = shift(low_before, *two), shift(high_after, -two[0], -two[1])
        blocks = (low, high), (low_after, high_after), (low_far, high_far), (low_before, high_before)
        gathered.append([jnp.concatenate(x, axis=0) for x in blocks])
    weights = jnp.concatenate([query_base_output, value_base_output], axis=1)
    partial = []
    for part in range(2):
        w = weights[part * half : (part + 1) * half]
        partial.append(
            jnp.stack(
                [
                    jnp.dot(x, w, preferred_element_type=F32).reshape(side, row_count, both)
                    for x in gathered[part]
                ]
            )
        )
    place = lax.axis_index("tp")
    projected = (partial[0] + jnp.swapaxes(partial[1], 0, 1)).astype(BF)
    projected = to_absolute(projected, place // side)
    projected = jnp.swapaxes(to_absolute(jnp.swapaxes(projected, 0, 1), place % side), 0, 1)
    projected, back = lax.optimization_barrier((projected, back))
    back = back.reshape(slot_total, back.shape[2])
    row_terms = jnp.dot(pick_table.T, back, preferred_element_type=F32).astype(BF)
    plain = lax.all_to_all(
        projected.reshape(members, row_count, both), "tp", split_axis=0, concat_axis=0, tiled=True
    )
    queries, values = finish(plain, row_terms, query_cols, value_cols)
    return (queries, values)


def solution(mesh):
    return jax.shard_map(
        on_device,
        mesh=mesh,
        in_specs=(
            P(("grp", "tp"), None),
            P(("grp", "tp"), None),
            P(("grp", "tp"), None),
            P(None, "tp"),
            P(None, "tp"),
            P(("grp", "tp"), None, None),
            P(("grp", "tp"), None, None),
            P(("grp", "tp"), None, None),
        ),
        out_specs=(P(("grp", "tp"), None), P(("grp", "tp"), None)),
        check_vma=False,
    )
```

```python
import jax
import jax.numpy as jnp
from jax import lax
from jax.experimental import pallas as pl
from jax.experimental.pallas import tpu as pltpu
from jax.sharding import PartitionSpec as P

adapter_scale = 2.0
BF = jnp.bfloat16
F32 = jnp.float32
side = 4


def shift(x, dy, dz):
    pairs = [
        (y * side + z, (y + dy) % side * side + (z + dz) % side)
        for y in range(side)
        for z in range(side)
    ]
    return lax.ppermute(x, "tp", pairs)


def line_sides(x, step):
    return shift(x, -step[0], -step[1]), shift(x, *step)


def line_far(after, before, step):
    half = before.shape[0] // 2
    return shift(before[:half], *step), shift(after[half:], -step[0], -step[1])


def line_gather(x, step):
    after, before = line_sides(x, step)
    return after, line_far(after, before, step), before


def to_absolute(blocks, place):
    for bit in (1, 2):
        moved = jnp.roll(blocks, bit, axis=0)
        blocks = jnp.where((place & bit) != 0, moved, blocks)
    return blocks


def apply_lowrank_adapters(rows, choice, adapter_down_weight, adapter_query_up, adapter_value_up):
    rank = adapter_query_up.shape[1]
    count = adapter_down_weight.shape[0]
    query_parts, value_parts = [], []
    for i in range(count):
        reduced = jnp.dot(rows, adapter_down_weight[i], preferred_element_type=F32)
        reduced = jnp.where(choice == i, reduced, 0.0).astype(BF)
        query_parts.append(reduced[:, :rank])
        value_parts.append(reduced[:, rank:])
    query_low = jnp.concatenate(query_parts, axis=1)
    value_low = jnp.concatenate(value_parts, axis=1)
    query_up = adapter_query_up.reshape(count * rank, adapter_query_up.shape[2])
    value_up = adapter_value_up.reshape(count * rank, adapter_value_up.shape[2])
    query = (adapter_scale * jnp.dot(query_low, query_up, preferred_element_type=F32)).astype(BF)
    value = (adapter_scale * jnp.dot(value_low, value_up, preferred_element_type=F32)).astype(BF)
    return query, value


def finish_kernel(plain_ref, term_ref, queries_ref, values_ref):
    members, _, both = plain_ref.shape
    query_cols = queries_ref.shape[1] // members
    value_cols = both - query_cols
    for i in range(members):
        cols = slice(i * query_cols, (i + 1) * query_cols)
        base = plain_ref[i, :, :query_cols].astype(F32)
        queries_ref[:, cols] = (base + term_ref[:, cols].astype(F32)).astype(BF)
    at = members * query_cols
    for i in range(0, members, 2):
        base = jnp.concatenate([plain_ref[i, :, query_cols:], plain_ref[i + 1, :, query_cols:]], axis=1)
        cols = slice(i * value_cols, (i + 2) * value_cols)
        term = term_ref[:, at + i * value_cols : at + (i + 2) * value_cols].astype(F32)
        values_ref[:, cols] = (base.astype(F32) + term).astype(BF)


def finish(plain, terms, query_cols, value_cols):
    members, rows, both = plain.shape
    whole = pl.BlockSpec(memory_space=pltpu.VMEM)
    return pl.pallas_call(
        finish_kernel,
        in_specs=[whole, whole],
        out_specs=[whole, whole],
        out_shape=[
            jax.ShapeDtypeStruct((rows, members * query_cols), BF),
            jax.ShapeDtypeStruct((rows, members * value_cols), BF),
        ],
        compiler_params=pltpu.CompilerParams(vmem_limit_bytes=24 << 20),
        cost_estimate=pl.CostEstimate(
            flops=rows * members * both, bytes_accessed=6 * rows * members * both, transcendentals=0
        ),
    )(plain, terms)


def on_device(
    tokens,
    holder,
    adapter_choice_index,
    query_base_output,
    value_base_output,
    adapter_down_weight,
    adapter_query_up,
    adapter_value_up,
):
    row_count, width = tokens.shape
    query_cols = query_base_output.shape[1]
    value_cols = value_base_output.shape[1]
    both = query_cols + value_cols
    members = lax.axis_size("tp")
    devices = lax.axis_size("grp") * members
    capacity = 2
    slot_total = devices * capacity

    holder_id = holder[:, 0]
    same_holder = holder_id[:, None] == holder_id[None, :]
    index = jnp.arange(row_count, dtype=jnp.int32)
    earlier = index[:, None] > index[None, :]
    position = jnp.sum((same_holder & earlier).astype(jnp.int32), axis=1)
    slot_index = holder_id * capacity + position
    pick_table = (jnp.arange(slot_total, dtype=jnp.int32)[:, None] == slot_index[None, :]).astype(BF)
    marked = jnp.concatenate(
        [tokens, jnp.broadcast_to(adapter_choice_index.astype(BF), (row_count, 128))], axis=1
    )
    send_rows = jnp.dot(pick_table, marked, preferred_element_type=F32).astype(BF)
    send_rows = send_rows.reshape(devices, capacity, width + 128)

    got_rows = lax.all_to_all(
        send_rows, ("grp", "tp"), split_axis=0, concat_axis=0, tiled=True
    ).reshape(slot_total, width + 128)
    query_term, value_term = apply_lowrank_adapters(
        got_rows[:, :width],
        got_rows[:, width : width + 1],
        adapter_down_weight,
        adapter_query_up,
        adapter_value_up,
    )
    terms = jnp.concatenate([query_term, value_term], axis=1)
    back = lax.all_to_all(
        terms.reshape(devices, capacity, terms.shape[1]),
        ("grp", "tp"),
        split_axis=0,
        concat_axis=0,
        tiled=True,
    )

    half = width // 2
    along_z, along_y = (0, 1), (1, 0)
    gathered = []
    for part, (one, two) in enumerate(((along_z, along_y), (along_y, along_z))):
        own = tokens[:, part * half : (part + 1) * half]
        after, far, before = line_gather(own, one)
        line = jnp.concatenate([own, after, *far, before], axis=0)
        after, before = line_sides(line, two)
        gathered.append([line, after, before])
    weights = jnp.concatenate([query_base_output, value_base_output], axis=1)
    for blocks, two in zip(gathered, (along_y, along_z)):
        blocks.insert(2, jnp.concatenate(line_far(blocks[1], blocks[2], two), axis=0))
    partial = []
    for part in range(2):
        w = weights[part * half : (part + 1) * half]
        partial.append(
            jnp.stack(
                [
                    jnp.dot(x, w, preferred_element_type=F32).reshape(side, row_count, both)
                    for x in gathered[part]
                ]
            )
        )
    place = lax.axis_index("tp")
    projected = (partial[0] + jnp.swapaxes(partial[1], 0, 1)).astype(BF)
    projected = to_absolute(projected, place // side)
    projected = jnp.swapaxes(to_absolute(jnp.swapaxes(projected, 0, 1), place % side), 0, 1)
    projected, back = lax.optimization_barrier((projected, back))
    back = back.reshape(slot_total, back.shape[2])
    row_terms = jnp.dot(pick_table.T, back, preferred_element_type=F32).astype(BF)
    plain = lax.all_to_all(
        projected.reshape(members, row_count, both), "tp", split_axis=0, concat_axis=0, tiled=True
    )
    queries, values = finish(plain, row_terms, query_cols, value_cols)
    return (queries, values)


def solution(mesh):
    return jax.shard_map(
        on_device,
        mesh=mesh,
        in_specs=(
            P(("grp", "tp"), None),
            P(("grp", "tp"), None),
            P(("grp", "tp"), None),
            P(None, "tp"),
            P(None, "tp"),
            P(("grp", "tp"), None, None),
            P(("grp", "tp"), None, None),
            P(("grp", "tp"), None, None),
        ),
        out_specs=(P(("grp", "tp"), None), P(("grp", "tp"), None)),
        check_vma=False,
    )
```

```python
import jax
import jax.numpy as jnp
from jax import lax
from jax.experimental import pallas as pl
from jax.experimental.pallas import tpu as pltpu
from jax.sharding import PartitionSpec as P

adapter_scale = 2.0
BF = jnp.bfloat16
F32 = jnp.float32
side = 4


def shift(x, dy, dz):
    pairs = [
        (y * side + z, (y + dy) % side * side + (z + dz) % side)
        for y in range(side)
        for z in range(side)
    ]
    return lax.ppermute(x, "tp", pairs)


def line_sides(x, step):
    return shift(x, -step[0], -step[1]), shift(x, *step)


def line_far(after, before, step):
    half = before.shape[0] // 2
    return shift(before[:half], *step), shift(after[half:], -step[0], -step[1])


def to_absolute(blocks, place):
    for bit in (1, 2):
        moved = jnp.roll(blocks, bit, axis=0)
        blocks = jnp.where((place & bit) != 0, moved, blocks)
    return blocks


def apply_lowrank_adapters(rows, choice, adapter_down_weight, adapter_query_up, adapter_value_up):
    rank = adapter_query_up.shape[1]
    count = adapter_down_weight.shape[0]
    query_parts, value_parts = [], []
    for i in range(count):
        reduced = jnp.dot(rows, adapter_down_weight[i], preferred_element_type=F32)
        reduced = jnp.where(choice == i, reduced, 0.0).astype(BF)
        query_parts.append(reduced[:, :rank])
        value_parts.append(reduced[:, rank:])
    query_low = jnp.concatenate(query_parts, axis=1)
    value_low = jnp.concatenate(value_parts, axis=1)
    query_up = adapter_query_up.reshape(count * rank, adapter_query_up.shape[2])
    value_up = adapter_value_up.reshape(count * rank, adapter_value_up.shape[2])
    query = (adapter_scale * jnp.dot(query_low, query_up, preferred_element_type=F32)).astype(BF)
    value = (adapter_scale * jnp.dot(value_low, value_up, preferred_element_type=F32)).astype(BF)
    return query, value


def finish_kernel(plain_ref, term_ref, queries_ref, values_ref):
    members, _, both = plain_ref.shape
    query_cols = queries_ref.shape[1] // members
    value_cols = both - query_cols
    for i in range(members):
        cols = slice(i * query_cols, (i + 1) * query_cols)
        base = plain_ref[i, :, :query_cols].astype(F32)
        queries_ref[:, cols] = (base + term_ref[:, cols].astype(F32)).astype(BF)
    at = members * query_cols
    for i in range(0, members, 2):
        base = jnp.concatenate([plain_ref[i, :, query_cols:], plain_ref[i + 1, :, query_cols:]], axis=1)
        cols = slice(i * value_cols, (i + 2) * value_cols)
        term = term_ref[:, at + i * value_cols : at + (i + 2) * value_cols].astype(F32)
        values_ref[:, cols] = (base.astype(F32) + term).astype(BF)


def finish(plain, terms, query_cols, value_cols):
    members, rows, both = plain.shape
    whole = pl.BlockSpec(memory_space=pltpu.VMEM)
    return pl.pallas_call(
        finish_kernel,
        in_specs=[whole, whole],
        out_specs=[whole, whole],
        out_shape=[
            jax.ShapeDtypeStruct((rows, members * query_cols), BF),
            jax.ShapeDtypeStruct((rows, members * value_cols), BF),
        ],
        compiler_params=pltpu.CompilerParams(vmem_limit_bytes=24 << 20),
        cost_estimate=pl.CostEstimate(
            flops=rows * members * both, bytes_accessed=6 * rows * members * both, transcendentals=0
        ),
    )(plain, terms)


def on_device(
    tokens,
    holder,
    adapter_choice_index,
    query_base_output,
    value_base_output,
    adapter_down_weight,
    adapter_query_up,
    adapter_value_up,
):
    row_count, width = tokens.shape
    query_cols = query_base_output.shape[1]
    value_cols = value_base_output.shape[1]
    both = query_cols + value_cols
    members = lax.axis_size("tp")
    devices = lax.axis_size("grp") * members
    capacity = 2
    slot_total = devices * capacity

    holder_id = holder[:, 0]
    same_holder = holder_id[:, None] == holder_id[None, :]
    index = jnp.arange(row_count, dtype=jnp.int32)
    earlier = index[:, None] > index[None, :]
    position = jnp.sum((same_holder & earlier).astype(jnp.int32), axis=1)
    slot_index = holder_id * capacity + position
    pick_table = (jnp.arange(slot_total, dtype=jnp.int32)[:, None] == slot_index[None, :]).astype(BF)
    marked = jnp.concatenate(
        [tokens, jnp.broadcast_to(adapter_choice_index.astype(BF), (row_count, 128))], axis=1
    )
    send_rows = jnp.dot(pick_table, marked, preferred_element_type=F32).astype(BF)
    send_rows = send_rows.reshape(devices, capacity, width + 128)

    half = width // 2
    along_z, along_y = (0, 1), (1, 0)
    owns = [tokens[:, part * half : (part + 1) * half] for part in range(2)]
    nexts = [line_sides(own, one) for own, one in zip(owns, (along_z, along_y))]
    nexts, send_rows = lax.optimization_barrier((nexts, send_rows))
    got_rows = lax.all_to_all(
        send_rows, ("grp", "tp"), split_axis=0, concat_axis=0, tiled=True
    ).reshape(slot_total, width + 128)
    query_term, value_term = apply_lowrank_adapters(
        got_rows[:, :width],
        got_rows[:, width : width + 1],
        adapter_down_weight,
        adapter_query_up,
        adapter_value_up,
    )
    terms = jnp.concatenate([query_term, value_term], axis=1)
    terms = terms.reshape(devices, capacity, terms.shape[1])
    slot_index, terms = lax.optimization_barrier((slot_index, terms))
    back = lax.all_to_all(
        terms,
        ("grp", "tp"),
        split_axis=0,
        concat_axis=0,
        tiled=True,
    )

    n = row_count
    weights = jnp.concatenate([query_base_output, value_base_output], axis=1)
    partial = []
    for part, (one, two) in enumerate(((along_z, along_y), (along_y, along_z))):
        back_one = (-one[0], -one[1])
        own, (after, before) = owns[part], nexts[part]
        near = jnp.concatenate([own, after, before], axis=0)
        near_after, near_before = line_sides(near, two)
        near_after, near_before, slot_index = lax.optimization_barrier(
            (near_after, near_before, slot_index)
        )
        near_far = line_far(near_after, near_before, two)
        low = jnp.concatenate([before, near_after[2 * n :]], axis=0)
        cut = 3 * n // 2
        high = jnp.concatenate(
            [near_before[n : 2 * n], near_far[0][n:], near_far[1][: 2 * n - cut]], axis=0
        )
        far_low, far_high = shift(low, *one), shift(high, *back_one)

        w = weights[part * half : (part + 1) * half]

        def times(x):
            return jnp.dot(x, w, preferred_element_type=F32).reshape(-1, row_count, both)

        lines = [times(x) for x in (near, near_after, jnp.concatenate(near_far, axis=0))]
        if part == 1:
            near_before, back = lax.optimization_barrier((near_before, back))
        lines.append(times(near_before))
        far = times(jnp.concatenate([far_low, far_high], axis=0))
        partial.append(
            jnp.stack(
                [
                    jnp.stack([line[0], line[1], far[i], line[2]])
                    for line, i in zip(lines, (0, 1, 3, 2))
                ]
            )
        )
    place = lax.axis_index("tp")
    projected = (partial[0] + jnp.swapaxes(partial[1], 0, 1)).astype(BF)
    projected = to_absolute(projected, place // side)
    projected = jnp.swapaxes(to_absolute(jnp.swapaxes(projected, 0, 1), place % side), 0, 1)
    projected, back = lax.optimization_barrier((projected, back))
    back = back.reshape(slot_total, back.shape[2])
    pick_row = (slot_index[:, None] == jnp.arange(slot_total, dtype=jnp.int32)[None, :]).astype(BF)
    row_terms = jnp.dot(pick_row, back, preferred_element_type=F32).astype(BF)
    plain = lax.all_to_all(
        projected.reshape(members, row_count, both), "tp", split_axis=0, concat_axis=0, tiled=True
    )
    queries, values = finish(plain, row_terms, query_cols, value_cols)
    return (queries, values)


def solution(mesh):
    return jax.shard_map(
        on_device,
        mesh=mesh,
        in_specs=(
            P(("grp", "tp"), None),
            P(("grp", "tp"), None),
            P(("grp", "tp"), None),
            P(None, "tp"),
            P(None, "tp"),
            P(("grp", "tp"), None, None),
            P(("grp", "tp"), None, None),
            P(("grp", "tp"), None, None),
        ),
        out_specs=(P(("grp", "tp"), None), P(("grp", "tp"), None)),
        check_vma=False,
    )
```

```python
import jax
import jax.numpy as jnp
from jax import lax
from jax.experimental import pallas as pl
from jax.experimental.pallas import tpu as pltpu
from jax.sharding import PartitionSpec as P

adapter_scale = 2.0
BF = jnp.bfloat16
F32 = jnp.float32
side = 4


def shift(x, dy, dz):
    pairs = [
        (y * side + z, (y + dy) % side * side + (z + dz) % side)
        for y in range(side)
        for z in range(side)
    ]
    return lax.ppermute(x, "tp", pairs)


def line_sides(x, step):
    return shift(x, -step[0], -step[1]), shift(x, *step)


def line_far(after, before, step):
    half = before.shape[0] // 2
    return shift(before[:half], *step), shift(after[half:], -step[0], -step[1])


def line_gather(x, step):
    after, before = line_sides(x, step)
    return after, line_far(after, before, step), before


def to_absolute(blocks, place):
    for bit in (1, 2):
        moved = jnp.roll(blocks, bit, axis=0)
        blocks = jnp.where((place & bit) != 0, moved, blocks)
    return blocks


def apply_lowrank_adapters(rows, choice, adapter_down_weight, adapter_query_up, adapter_value_up):
    rank = adapter_query_up.shape[1]
    count = adapter_down_weight.shape[0]
    query_parts, value_parts = [], []
    for i in range(count):
        reduced = jnp.dot(rows, adapter_down_weight[i], preferred_element_type=F32)
        reduced = jnp.where(choice == i, reduced, 0.0).astype(BF)
        query_parts.append(reduced[:, :rank])
        value_parts.append(reduced[:, rank:])
    query_low = jnp.concatenate(query_parts, axis=1)
    value_low = jnp.concatenate(value_parts, axis=1)
    query_up = adapter_query_up.reshape(count * rank, adapter_query_up.shape[2])
    value_up = adapter_value_up.reshape(count * rank, adapter_value_up.shape[2])
    query = (adapter_scale * jnp.dot(query_low, query_up, preferred_element_type=F32)).astype(BF)
    value = (adapter_scale * jnp.dot(value_low, value_up, preferred_element_type=F32)).astype(BF)
    return query, value


def finish_kernel(plain_ref, term_ref, queries_ref, values_ref):
    members, _, both = plain_ref.shape
    query_cols = queries_ref.shape[1] // members
    value_cols = both - query_cols
    for i in range(members):
        cols = slice(i * query_cols, (i + 1) * query_cols)
        base = plain_ref[i, :, :query_cols].astype(F32)
        queries_ref[:, cols] = (base + term_ref[:, cols].astype(F32)).astype(BF)
    at = members * query_cols
    for i in range(0, members, 2):
        base = jnp.concatenate([plain_ref[i, :, query_cols:], plain_ref[i + 1, :, query_cols:]], axis=1)
        cols = slice(i * value_cols, (i + 2) * value_cols)
        term = term_ref[:, at + i * value_cols : at + (i + 2) * value_cols].astype(F32)
        values_ref[:, cols] = (base.astype(F32) + term).astype(BF)


def finish(plain, terms, query_cols, value_cols):
    members, rows, both = plain.shape
    whole = pl.BlockSpec(memory_space=pltpu.VMEM)
    return pl.pallas_call(
        finish_kernel,
        in_specs=[whole, whole],
        out_specs=[whole, whole],
        out_shape=[
            jax.ShapeDtypeStruct((rows, members * query_cols), BF),
            jax.ShapeDtypeStruct((rows, members * value_cols), BF),
        ],
        compiler_params=pltpu.CompilerParams(vmem_limit_bytes=24 << 20),
        cost_estimate=pl.CostEstimate(
            flops=rows * members * both, bytes_accessed=6 * rows * members * both, transcendentals=0
        ),
    )(plain, terms)


def on_device(
    tokens,
    holder,
    adapter_choice_index,
    query_base_output,
    value_base_output,
    adapter_down_weight,
    adapter_query_up,
    adapter_value_up,
):
    row_count, width = tokens.shape
    query_cols = query_base_output.shape[1]
    value_cols = value_base_output.shape[1]
    both = query_cols + value_cols
    members = lax.axis_size("tp")
    devices = lax.axis_size("grp") * members
    capacity = 2
    slot_total = devices * capacity

    holder_id = holder[:, 0]
    same_holder = holder_id[:, None] == holder_id[None, :]
    index = jnp.arange(row_count, dtype=jnp.int32)
    earlier = index[:, None] > index[None, :]
    position = jnp.sum((same_holder & earlier).astype(jnp.int32), axis=1)
    slot_index = holder_id * capacity + position
    pick_table = (jnp.arange(slot_total, dtype=jnp.int32)[:, None] == slot_index[None, :]).astype(BF)
    marked = jnp.concatenate(
        [tokens, jnp.broadcast_to(adapter_choice_index.astype(BF), (row_count, 128))], axis=1
    )
    send_rows = jnp.dot(pick_table, marked, preferred_element_type=F32).astype(BF)
    send_rows = send_rows.reshape(devices, capacity, width + 128)

    got_rows = lax.all_to_all(
        send_rows, ("grp", "tp"), split_axis=0, concat_axis=0, tiled=True
    ).reshape(slot_total, width + 128)
    query_term, value_term = apply_lowrank_adapters(
        got_rows[:, :width],
        got_rows[:, width : width + 1],
        adapter_down_weight,
        adapter_query_up,
        adapter_value_up,
    )
    terms = jnp.concatenate([query_term, value_term], axis=1)
    terms = terms.reshape(devices, capacity, terms.shape[1])
    weights = jnp.concatenate([query_base_output, value_base_output], axis=1)
    terms, weights = lax.optimization_barrier((terms, weights))
    back = lax.all_to_all(
        terms,
        ("grp", "tp"),
        split_axis=0,
        concat_axis=0,
        tiled=True,
    )

    half = width // 2
    along_z, along_y = (0, 1), (1, 0)
    gathered = []
    for part, (one, two) in enumerate(((along_z, along_y), (along_y, along_z))):
        own = tokens[:, part * half : (part + 1) * half]
        after, far, before = line_gather(own, one)
        line = jnp.concatenate([own, after, *far, before], axis=0)
        after, before = line_sides(line, two)
        gathered.append([line, after, before])
    for blocks, two in zip(gathered, (along_y, along_z)):
        blocks.insert(2, jnp.concatenate(line_far(blocks[1], blocks[2], two), axis=0))
    partial = []
    for part in range(2):
        w = weights[part * half : (part + 1) * half]
        partial.append(
            jnp.stack(
                [
                    jnp.dot(x, w, preferred_element_type=F32).reshape(side, row_count, both)
                    for x in gathered[part]
                ]
            )
        )
    place = lax.axis_index("tp")
    projected = (partial[0] + jnp.swapaxes(partial[1], 0, 1)).astype(BF)
    projected = to_absolute(projected, place // side)
    projected = jnp.swapaxes(to_absolute(jnp.swapaxes(projected, 0, 1), place % side), 0, 1)
    projected, back = lax.optimization_barrier((projected, back))
    back = back.reshape(slot_total, back.shape[2])
    row_terms = jnp.dot(pick_table.T, back, preferred_element_type=F32).astype(BF)
    plain = lax.all_to_all(
        projected.reshape(members, row_count, both), "tp", split_axis=0, concat_axis=0, tiled=True
    )
    queries, values = finish(plain, row_terms, query_cols, value_cols)
    return (queries, values)


def solution(mesh):
    return jax.shard_map(
        on_device,
        mesh=mesh,
        in_specs=(
            P(("grp", "tp"), None),
            P(("grp", "tp"), None),
            P(("grp", "tp"), None),
            P(None, "tp"),
            P(None, "tp"),
            P(("grp", "tp"), None, None),
            P(("grp", "tp"), None, None),
            P(("grp", "tp"), None, None),
        ),
        out_specs=(P(("grp", "tp"), None), P(("grp", "tp"), None)),
        check_vma=False,
    )
```

```python
import jax
import jax.numpy as jnp
from jax import lax
from jax.experimental import pallas as pl
from jax.experimental.pallas import tpu as pltpu
from jax.sharding import PartitionSpec as P

adapter_scale = 2.0
BF = jnp.bfloat16
F32 = jnp.float32
side = 4


def shift(x, dy, dz):
    pairs = [
        (y * side + z, (y + dy) % side * side + (z + dz) % side)
        for y in range(side)
        for z in range(side)
    ]
    return lax.ppermute(x, "tp", pairs)


def line_sides(x, step):
    return shift(x, -step[0], -step[1]), shift(x, *step)


def line_far(after, before, step):
    half = before.shape[0] // 2
    return shift(before[:half], *step), shift(after[half:], -step[0], -step[1])


def line_gather(x, step):
    after, before = line_sides(x, step)
    return after, line_far(after, before, step), before


def to_absolute(blocks, place):
    for bit in (1, 2):
        moved = jnp.roll(blocks, bit, axis=0)
        blocks = jnp.where((place & bit) != 0, moved, blocks)
    return blocks


def apply_lowrank_adapters(rows, choice, adapter_down_weight, adapter_query_up, adapter_value_up):
    rank = adapter_query_up.shape[1]
    count = adapter_down_weight.shape[0]
    query_parts, value_parts = [], []
    for i in range(count):
        reduced = jnp.dot(rows, adapter_down_weight[i], preferred_element_type=F32)
        reduced = jnp.where(choice == i, reduced, 0.0).astype(BF)
        query_parts.append(reduced[:, :rank])
        value_parts.append(reduced[:, rank:])
    query_low = jnp.concatenate(query_parts, axis=1)
    value_low = jnp.concatenate(value_parts, axis=1)
    query_up = adapter_query_up.reshape(count * rank, adapter_query_up.shape[2])
    value_up = adapter_value_up.reshape(count * rank, adapter_value_up.shape[2])
    query = (adapter_scale * jnp.dot(query_low, query_up, preferred_element_type=F32)).astype(BF)
    value = (adapter_scale * jnp.dot(value_low, value_up, preferred_element_type=F32)).astype(BF)
    return query, value


def finish_kernel(plain_ref, query_term_ref, value_term_ref, queries_ref, values_ref):
    count, _, both = plain_ref.shape
    query_cols = queries_ref.shape[1] // count
    value_cols = both - query_cols
    for i in range(count):
        cols = slice(i * query_cols, (i + 1) * query_cols)
        base = plain_ref[i, :, :query_cols].astype(F32)
        queries_ref[:, cols] = (base + query_term_ref[:, cols].astype(F32)).astype(BF)
    for i in range(0, count, 2):
        cols = slice(i * value_cols, (i + 2) * value_cols)
        base = jnp.concatenate([plain_ref[i, :, query_cols:], plain_ref[i + 1, :, query_cols:]], axis=1)
        values_ref[:, cols] = (base.astype(F32) + value_term_ref[:, cols].astype(F32)).astype(BF)


def finish(plain, terms, query_cols, value_cols):
    members, rows, both = plain.shape
    count = 4
    value_at = members * query_cols // (count * value_cols)
    return pl.pallas_call(
        finish_kernel,
        grid=(members // count,),
        in_specs=[
            pl.BlockSpec((count, rows, both), lambda i: (i, 0, 0)),
            pl.BlockSpec((rows, count * query_cols), lambda i: (0, i)),
            pl.BlockSpec((rows, count * value_cols), lambda i: (0, value_at + i)),
        ],
        out_specs=[
            pl.BlockSpec((rows, count * query_cols), lambda i: (0, i)),
            pl.BlockSpec((rows, count * value_cols), lambda i: (0, i)),
        ],
        out_shape=[
            jax.ShapeDtypeStruct((rows, members * query_cols), BF),
            jax.ShapeDtypeStruct((rows, members * value_cols), BF),
        ],
        compiler_params=pltpu.CompilerParams(vmem_limit_bytes=24 << 20),
        cost_estimate=pl.CostEstimate(
            flops=rows * members * both, bytes_accessed=6 * rows * members * both, transcendentals=0
        ),
    )(plain, terms, terms)


def on_device(
    tokens,
    holder,
    adapter_choice_index,
    query_base_output,
    value_base_output,
    adapter_down_weight,
    adapter_query_up,
    adapter_value_up,
):
    row_count, width = tokens.shape
    query_cols = query_base_output.shape[1]
    value_cols = value_base_output.shape[1]
    both = query_cols + value_cols
    members = lax.axis_size("tp")
    devices = lax.axis_size("grp") * members
    capacity = 2
    slot_total = devices * capacity

    holder_id = holder[:, 0]
    same_holder = holder_id[:, None] == holder_id[None, :]
    index = jnp.arange(row_count, dtype=jnp.int32)
    earlier = index[:, None] > index[None, :]
    position = jnp.sum((same_holder & earlier).astype(jnp.int32), axis=1)
    slot_index = holder_id * capacity + position
    pick_table = (jnp.arange(slot_total, dtype=jnp.int32)[:, None] == slot_index[None, :]).astype(BF)
    marked = jnp.concatenate(
        [tokens, jnp.broadcast_to(adapter_choice_index.astype(BF), (row_count, 128))], axis=1
    )
    send_rows = jnp.dot(pick_table, marked, preferred_element_type=F32).astype(BF)
    send_rows = send_rows.reshape(devices, capacity, width + 128)

    got_rows = lax.all_to_all(
        send_rows, ("grp", "tp"), split_axis=0, concat_axis=0, tiled=True
    ).reshape(slot_total, width + 128)
    query_term, value_term = apply_lowrank_adapters(
        got_rows[:, :width],
        got_rows[:, width : width + 1],
        adapter_down_weight,
        adapter_query_up,
        adapter_value_up,
    )
    terms = jnp.concatenate([query_term, value_term], axis=1)
    back = lax.all_to_all(
        terms.reshape(devices, capacity, terms.shape[1]),
        ("grp", "tp"),
        split_axis=0,
        concat_axis=0,
        tiled=True,
    )

    half = width // 2
    along_z, along_y = (0, 1), (1, 0)
    gathered = []
    for part, (one, two) in enumerate(((along_z, along_y), (along_y, along_z))):
        own = tokens[:, part * half : (part + 1) * half]
        after, far, before = line_gather(own, one)
        line = jnp.concatenate([own, after, *far, before], axis=0)
        after, before = line_sides(line, two)
        gathered.append([line, after, before])
    query_base_output, value_base_output, _ = lax.optimization_barrier(
        (query_base_output, value_base_output, far[0][:16, :128])
    )
    weights = jnp.concatenate([query_base_output, value_base_output], axis=1)
    for blocks, two in zip(gathered, (along_y, along_z)):
        blocks.insert(2, jnp.concatenate(line_far(blocks[1], blocks[2], two), axis=0))
    partial = []
    for part in range(2):
        w = weights[part * half : (part + 1) * half]
        partial.append(
            jnp.stack(
                [
                    jnp.dot(x, w, preferred_element_type=F32).reshape(side, row_count, both)
                    for x in gathered[part]
                ]
            )
        )
    place = lax.axis_index("tp")
    projected = (partial[0] + jnp.swapaxes(partial[1], 0, 1)).astype(BF)
    projected = to_absolute(projected, place // side)
    projected = jnp.swapaxes(to_absolute(jnp.swapaxes(projected, 0, 1), place % side), 0, 1)
    projected, back = lax.optimization_barrier((projected, back))
    back = back.reshape(slot_total, back.shape[2])
    row_terms = jnp.dot(pick_table.T, back, preferred_element_type=F32).astype(BF)
    plain = lax.all_to_all(
        projected.reshape(members, row_count, both), "tp", split_axis=0, concat_axis=0, tiled=True
    )
    queries, values = finish(plain, row_terms, query_cols, value_cols)
    return (queries, values)


def solution(mesh):
    return jax.shard_map(
        on_device,
        mesh=mesh,
        in_specs=(
            P(("grp", "tp"), None),
            P(("grp", "tp"), None),
            P(("grp", "tp"), None),
            P(None, "tp"),
            P(None, "tp"),
            P(("grp", "tp"), None, None),
            P(("grp", "tp"), None, None),
            P(("grp", "tp"), None, None),
        ),
        out_specs=(P(("grp", "tp"), None), P(("grp", "tp"), None)),
        check_vma=False,
    )
```
